512 devices in a mesh: lev: 16 (over y, x_lo, core), lat: 32 (over x_hi, z).
Axes of the slice: x: 4 (x_hi: 2, x_lo: 2; x = x_hi * 2 + x_lo), y: 4, z: 16, core: 2. Of those that a mesh axis runs over, the one named last changes fastest.
Arguments:
- tokens: bfloat16 [32, 192, 192, 512], P('lev', 'lat'), may hold values from -6 to 6
- latent_query: bfloat16 [3, 1024], replicated, may hold values from -48 to 48
- latent_base: bfloat16 [3, 512], replicated, may hold values from -6 to 6
- key_weight: bfloat16 [512, 1024], P('lat'), may hold values from -0.25 to 0.25
- value_weight: bfloat16 [512, 1024], P('lat'), may hold values from -0.25 to 0.25
- out_weight: bfloat16 [1024, 512], P('lat'), may hold values from -0.1875 to 0.1875
- norm_gain: float32 [512], replicated, may hold values from 0.1 to 1.9
- window_qkv: bfloat16 [512, 1536], P('lat'), may hold values from -0.25 to 0.25
- window_proj: bfloat16 [512, 512], P('lat'), may hold values from -0.25 to 0.25
Outputs:
- section_out: bfloat16 [3, 192, 192, 512], P(None, 'lat', 'lev')
The draws below stay inside these ranges and needn't reach their ends.
All inputs are finite; a program needn't handle non-finite values.
Results may differ from the reference program's by a relative error of at most 0.011.
Values may be sent and summed in bfloat16 or wider, within the bound.
A program may use at most 192 MiB of HBM per device.

```python
import math
import jax
import jax.numpy as jnp
from jax import lax

D = 512
HEAD_DIM = 64
LHEADS = 16
INNER = 1024
LATENTS = 3
LEVELS = 32
WIN_R = 6
WIN_C = 12
ROWS_DEV = 6
NR = 192
NC = 192
N_LAT = 32


def draw_latent_query(key, part):
    key = jax.random.fold_in(key, 7)
    first = jax.random.fold_in(key, 0)
    base = jax.random.normal(first, (LATENTS, INNER), jnp.float32)
    return jnp.clip(base * 2.0, -8.0, 8.0).astype(jnp.bfloat16)


def shard_levels(rng, dims, cuts, smallest, top_value):
    factor_of, own = 1.0, jax.random.fold_in(rng, 6)
    for position, parts in cuts:
        heights = jnp.exp(jax.random.uniform(jax.random.fold_in(own, position), (parts,), jnp.float32, smallest / len(cuts), top_value / len(cuts)))
        factor_of = factor_of * jnp.repeat(heights, dims[position] // parts).reshape([-1 if axis == position else 1 for axis in range(len(dims))])
    return factor_of


def centred(own_key, dims, scale, most, cuts=(), kind=jnp.bfloat16):
    loudness = shard_levels(own_key, dims, cuts, -0.22, 0.18) if cuts else 1.0
    values = jax.random.normal(own_key, dims, jnp.float32) * scale * loudness
    return jnp.minimum(jnp.maximum(values, -most), most).astype(kind)


def setup_inputs(seed: int = 0) -> dict:
    key_list = jax.random.split(jax.random.key(seed), 10)
    return {
        "tokens": centred(key_list[0], (LEVELS, NR, NC, D), 1.0, 6.0, ((0, 16), (1, 32))),
        "latent_query": draw_latent_query(jax.random.fold_in(key_list[9], 71), 0),
        "latent_base": centred(key_list[2], (LATENTS, D), 1.0, 6.0),
        "key_weight": centred(key_list[3], (D, INNER), D ** -0.5, 0.25, ((0, 32),)),
        "value_weight": centred(key_list[4], (D, INNER), D ** -0.5, 0.25, ((0, 32),)),
        "out_weight": centred(key_list[5], (INNER, D), INNER ** -0.5, 0.1875, ((0, 32),)),
        "norm_gain": jnp.clip(1.0 + 0.18 * jax.random.normal(key_list[6], (D,), jnp.float32), 0.1, 1.9),
        "window_qkv": centred(key_list[7], (D, 3 * D), D ** -0.5, 0.25, ((0, 32),)),
        "window_proj": centred(key_list[8], (D, D), D ** -0.5, 0.25, ((0, 32),)),
    }


def layer_norm(values, norm_gain):
    floats = values.astype(jnp.float32)
    center = lax.optimization_barrier(jnp.mean(floats, axis=-1, keepdims=True))
    spread = lax.optimization_barrier(jnp.mean((floats - center) ** 2, axis=-1, keepdims=True))
    return ((floats - center) * lax.rsqrt(spread + 1e-05) * norm_gain).astype(jnp.bfloat16)

def level_attention(band_tokens, latent_query, latent_base, key_weight, value_weight, out_weight):
    levels, rows, cols, width = band_tokens.shape
    inner = key_weight.shape[1]
    head_dim = inner // LHEADS
    key_rows = jnp.dot(band_tokens, key_weight, preferred_element_type=jnp.float32).astype(jnp.bfloat16)
    value_rows = jnp.dot(band_tokens, value_weight, preferred_element_type=jnp.float32).astype(jnp.bfloat16)
    key_rows = key_rows.astype(jnp.float32).reshape(levels, rows, cols, LHEADS, head_dim)
    value_rows = value_rows.astype(jnp.float32).reshape(levels, rows, cols, LHEADS, head_dim)
    queries = latent_query.astype(jnp.float32).reshape(LATENTS, LHEADS, head_dim)
    scores = jnp.einsum('lhe,trche->ltrch', queries, key_rows) / math.sqrt(head_dim)
    maxima = lax.optimization_barrier(jnp.max(scores, axis=1))
    weights = jnp.exp(scores - maxima[:, None])
    totals = lax.optimization_barrier(jnp.sum(weights, axis=1))
    numerator = jnp.einsum('ltrch,trche->lrche', weights, value_rows)
    attn = (numerator / totals[..., None]).reshape(LATENTS, rows, cols, inner).astype(jnp.bfloat16)
    mixed = latent_base.astype(jnp.float32)[:, None, None, :] + jnp.dot(attn, out_weight, preferred_element_type=jnp.float32)
    return mixed.astype(jnp.bfloat16)

def window_attention(windows, allowed, norm_gain, window_qkv, window_proj):
    count, length, width = windows.shape
    heads = width // HEAD_DIM
    normed = layer_norm(windows, norm_gain)
    packed = jnp.dot(normed, window_qkv, preferred_element_type=jnp.float32).astype(jnp.bfloat16)
    queries = packed[..., :width].astype(jnp.float32).reshape(count, length, heads, HEAD_DIM)
    keys_all = packed[..., width:2 * width].astype(jnp.float32).reshape(count, length, heads, HEAD_DIM)
    values_all = packed[..., 2 * width:].astype(jnp.float32).reshape(count, length, heads, HEAD_DIM)
    scores = jnp.einsum('wihe,wjhe->whij', queries, keys_all) / math.sqrt(HEAD_DIM)
    scores = jnp.where(allowed, scores, -jnp.inf)
    peak = lax.optimization_barrier(jnp.max(scores, axis=-1, keepdims=True))
    weights = jnp.exp(scores - peak)
    wprobs = (weights / lax.optimization_barrier(jnp.sum(weights, axis=-1, keepdims=True))).astype(jnp.bfloat16)
    wout = jnp.einsum('whij,wjhe->wihe', wprobs.astype(jnp.float32), values_all).astype(jnp.bfloat16)
    wout = wout.reshape(count, length, width)
    result = windows.astype(jnp.float32) + jnp.dot(wout, window_proj, preferred_element_type=jnp.float32)
    return result.astype(jnp.bfloat16)

def reference(tokens, latent_query, latent_base, key_weight, value_weight, out_weight, norm_gain, window_qkv, window_proj):

    def one_band(index):
        start = (index * ROWS_DEV).astype(jnp.int32)
        band_tokens = lax.dynamic_slice_in_dim(tokens, start, ROWS_DEV, 1)
        return level_attention(band_tokens, latent_query, latent_base, key_weight, value_weight, out_weight)
    bands = lax.map(one_band, jnp.arange(N_LAT, dtype=jnp.int32))
    latents = bands.transpose(1, 0, 2, 3, 4).reshape(LATENTS, NR, NC, D)
    shifted = jnp.roll(latents, (-(WIN_R // 2), -(WIN_C // 2)), axis=(1, 2))
    win_rows = NR // WIN_R
    win_cols = NC // WIN_C
    length = LATENTS * WIN_R * WIN_C
    windows = shifted.reshape(LATENTS, win_rows, WIN_R, win_cols, WIN_C, D)
    windows = windows.transpose(1, 3, 0, 2, 4, 5).reshape(win_rows, win_cols, length, D)
    local_rows = jnp.broadcast_to(jnp.arange(WIN_R, dtype=jnp.int32)[None, :, None], (LATENTS, WIN_R, WIN_C)).reshape(length)

    def one_row(inputs):
        row_windows, index = inputs
        region = index * WIN_R + local_rows >= NR - WIN_R // 2
        allowed = (region[:, None] == region[None, :])[None, None]
        return window_attention(row_windows, allowed, norm_gain, window_qkv, window_proj)
    done = lax.map(one_row, (windows, jnp.arange(win_rows, dtype=jnp.int32)))
    done = done.reshape(win_rows, win_cols, LATENTS, WIN_R, WIN_C, D).transpose(2, 0, 3, 1, 4, 5)
    return done.reshape(LATENTS, NR, NC, D)
```

```python
import functools

import jax
import jax.numpy as jnp
from jax import lax
from jax.experimental import pallas as pl
from jax.experimental.pallas import tpu as pltpu
from jax.sharding import PartitionSpec as P

MESH = pl.DeviceIdType.MESH
F32 = jnp.float32
BF16 = jnp.bfloat16

HEAD_DIM = 64
LHEADS = 16
LATENTS = 3
WIN_R = 6
WIN_C = 12
WIDTH = 512
INNER = 1024
PATCHES = WIN_R * WIN_C
SHARD = 16
C_Q, C_V, C_O, C_W, C_P, C_END = 0, 128, 640, 1152, 1920, 2176


def dot(a, b):
    return jnp.dot(a, b, preferred_element_type=F32)


def dot_t(a, b):
    return lax.dot_general(a, b, (((1,), (1,)), ((), ())), preferred_element_type=F32)


def iota(shape, dim):
    return lax.broadcasted_iota(jnp.int32, shape, dim)


def pack_weights(mine, q_ref, kw_ref, vw_ref, ow_ref, qkvw_ref, pw_ref, gathered):
    own_head = iota((LHEADS, INNER), 0) == iota((LHEADS, INNER), 1) // HEAD_DIM
    spread = [
        jnp.where(own_head, q_ref[l : l + 1, :].astype(F32), 0.0) for l in range(LATENTS)
    ]
    spread.append(jnp.zeros((128 - LATENTS * LHEADS, INNER), F32))
    spread = jnp.concatenate(spread, axis=0).astype(BF16)
    folded = dot_t(kw_ref[...], spread) * (HEAD_DIM**-0.5)
    high = folded.astype(BF16)
    parts = (high, (folded - high.astype(F32)).astype(BF16))
    for c in range(2):
        gathered[mine, c, :, C_Q:C_V] = parts[c]
        gathered[mine, c, :, C_V:C_O] = vw_ref[:, c * 512 : c * 512 + 512]
        gathered[mine, c, :, C_O:C_W] = ow_ref[c * 16 : c * 16 + 16, :]
        gathered[mine, c, :, C_W:C_P] = qkvw_ref[:, c * 768 : c * 768 + 768]
        gathered[mine, c, :, C_P:C_END] = pw_ref[:, c * 256 : c * 256 + 256]


def regroup_tokens(group, devices, token_rows, floats, outgoing):
    cols = devices * WIN_C
    for k in range(4):
        floats[k, 0:cols] = token_rows[4 * group + k].astype(F32)
        floats[k, cols : cols + 8] = token_rows[4 * group + k, 0:16].astype(F32)[0:8]
    for i in range(devices):
        first = i * WIN_C + WIN_C // 2
        cut = [floats[k, first : first + WIN_C] for k in range(4)]
        outgoing[i, 48 * group : 48 * group + 48] = jnp.concatenate(cut, axis=0).astype(BF16)


def project_levels(g, arrived, gathered, scores, values):
    rows = arrived[pl.ds(g * 4, 4)].reshape(4 * 144, WIDTH)
    folded = jnp.concatenate(
        [gathered[:, c, :, C_Q:C_V].reshape(WIDTH, 128) for c in range(2)], axis=1
    )
    both = dot(rows, folded)
    scores[g] = both[:, :128] + both[:, 128:]
    for c in range(2):
        weight = gathered[:, c, :, C_V:C_O].reshape(WIDTH, 512)
        values[g, :, c * 512 : c * 512 + 512] = dot(rows, weight).astype(BF16)


def level_attention(scores, probs, values, attn):
    groups = scores.shape[0]

    def level(g):
        return scores[g].reshape(8, PATCHES, 128)

    peak = functools.reduce(jnp.maximum, [jnp.max(level(g), axis=0) for g in range(groups)])
    total = jnp.zeros((PATCHES, 128), F32)
    for g in range(groups):
        weights = jnp.exp(level(g) - peak[None])
        total = total + jnp.sum(weights, axis=0)
        scores[g] = weights.reshape(8 * PATCHES, 128)
    scale = 1.0 / total
    for g in range(groups):
        p = (level(g) * scale[None]).reshape(8 * PATCHES, 128)
        high = p.astype(BF16)
        probs[g, :, 0:128] = high
        probs[g, :, 128:256] = (p - high.astype(F32)).astype(BF16)
    head_of = lax.rem(iota((256, 256), 0), 128) - iota((256, 256), 1) // HEAD_DIM
    for l in range(LATENTS):
        for ch in range(INNER // 256):
            one_hot = jnp.where(head_of == l * LHEADS + ch * 4, 1.0, 0.0).astype(BF16)
            acc = jnp.zeros((PATCHES, 256), F32)
            for g in range(groups):
                wide = dot(probs[g], one_hot)
                v = values[g, :, ch * 256 : ch * 256 + 256].astype(F32)
                acc = acc + jnp.sum((wide * v).reshape(8, PATCHES, 256), axis=0)
            attn[l * PATCHES : (l + 1) * PATCHES, ch * 256 : ch * 256 + 256] = acc


def make_latents(attn, base_ref, gathered, latents):
    weight = gathered[:, :, :, C_O:C_W].reshape(INNER, WIDTH)
    mixed = dot(attn[...].astype(BF16), weight).reshape(LATENTS, PATCHES, WIDTH)
    for l in range(LATENTS):
        row = mixed[l] + base_ref[l : l + 1, :].astype(F32)
        latents[l] = row.astype(BF16).astype(F32)


def window_attention(last, window, gain_ref, gathered, packed, mixed, done, out_ref):
    length = LATENTS * PATCHES
    x = window[...]
    center = jnp.mean(x, axis=-1, keepdims=True)
    moved = x - center
    spread = jnp.mean(moved * moved, axis=-1, keepdims=True)
    normed = (moved * lax.rsqrt(spread + 1e-05) * gain_ref[...]).astype(BF16)
    for c in range(2):
        weight = gathered[:, c, :, C_W:C_P].reshape(WIDTH, 768)
        packed[:, c * 768 : c * 768 + 768] = dot(normed, weight).astype(BF16)
    half = PATCHES // 2

    def region(dim):
        return lax.rem(iota((length, length), dim), PATCHES) >= half

    apart = jnp.logical_and(region(0) != region(1), last)
    bias = jnp.where(apart, -1e30, 0.0)
    first = iota((length, 128), 1) < HEAD_DIM
    for pair in range(WIDTH // 128):
        at = pair * 128
        q = packed[:, at : at + 128].astype(F32) * (HEAD_DIM**-0.5)
        k = packed[:, WIDTH + at : WIDTH + at + 128]
        v = packed[:, 2 * WIDTH + at : 2 * WIDTH + at + 128]
        outs = []
        for side in (first, jnp.logical_not(first)):
            s = dot_t(jnp.where(side, q, 0.0).astype(BF16), k) + bias
            w = jnp.exp(s - jnp.max(s, axis=-1, keepdims=True))
            w = (w / jnp.sum(w, axis=-1, keepdims=True)).astype(BF16)
            outs.append(dot(w, v))
        mixed[:, at : at + 128] = jnp.where(first, outs[0], outs[1]).astype(BF16)
    for c in range(2):
        weight = gathered[:, c, :, C_P:C_END].reshape(WIDTH, 256)
        done[:, c * 256 : c * 256 + 256] = x[:, c * 256 : c * 256 + 256] + dot(mixed[...], weight)
    for l in range(LATENTS):
        for r in range(WIN_R):
            at = l * PATCHES + r * WIN_C
            out_ref[l, r] = done[at : at + WIN_C, :].astype(BF16)


def kernel(
    n_lev,
    n_lat,
    tok_ref,
    q_ref,
    base_ref,
    kw_ref,
    vw_ref,
    ow_ref,
    gain_ref,
    qkvw_ref,
    pw_ref,
    out_ref,
    gathered,
    arrived,
    outgoing,
    token_rows,
    floats,
    scores,
    probs,
    values,
    attn,
    latents,
    edge_out,
    edge_in,
    window,
    packed,
    mixed,
    done,
    load_sem,
    own_sem,
    tok_send,
    tok_recv,
    ring_send,
    ring_recv,
    core_send,
    core_recv,
    hop_sems,
    edge_sems,
):
    load = pltpu.make_async_copy(tok_ref, token_rows, load_sem)
    load.start()
    lev, lat = lax.axis_index("lev"), lax.axis_index("lat")
    depth = n_lat // 2
    side, z = lax.div(lat, depth), lax.rem(lat, depth)
    core = lax.rem(lev, 2)
    sibling = lev + 1 - 2 * core

    def at_z(step):
        return lax.rem(z + step + depth, depth)

    up, down = side * depth + at_z(1), side * depth + at_z(-1)
    across = (1 - side) * depth + z
    north, south = lax.rem(lat + n_lat - 1, n_lat), lax.rem(lat + 1, n_lat)

    barrier = pltpu.get_barrier_semaphore()
    for peer in (up, down, across, north, south):
        pl.semaphore_signal(
            barrier, inc=1, device_id={"lev": lev, "lat": peer}, device_id_type=MESH
        )
    for k in range(1, n_lev):
        peer = lax.rem(lev + k, n_lev)
        pl.semaphore_signal(
            barrier, inc=1, device_id={"lev": peer, "lat": lat}, device_id_type=MESH
        )
    pack_weights(lat, q_ref, kw_ref, vw_ref, ow_ref, qkvw_ref, pw_ref, gathered)
    pl.semaphore_wait(barrier, 5 + n_lev - 1)

    def share(shard, half, send, recv, to_lev, to_lat):
        return pltpu.make_async_remote_copy(
            src_ref=gathered.at[shard, half],
            dst_ref=gathered.at[shard, half],
            send_sem=send,
            recv_sem=recv,
            device_id={"lev": to_lev, "lat": to_lat},
            device_id_type=MESH,
        )

    steps = (depth // 2, depth - 1 - depth // 2)

    def shard_at(stream, step):
        return (side if stream == 0 else 1 - side) * depth + at_z(step)

    def ring(way, stream, step, arriving):
        far = step if arriving else step - 1
        shard = shard_at(stream, -far if way == 0 else far)
        where = (way * 2 + stream) * steps[0] + step - 1
        return share(
            shard, core, ring_send.at[where], ring_recv.at[where], lev, up if way == 0 else down
        )

    def to_sibling(shard):
        return share(shard, core, core_send.at[shard], core_recv.at[shard], sibling, lat)

    def from_sibling(shard):
        return share(shard, 1 - core, core_send.at[shard], core_recv.at[shard], sibling, lat)

    crossing = share(lat, core, hop_sems.at[0], hop_sems.at[1], lev, across)
    crossed = share(across, core, hop_sems.at[0], hop_sems.at[1], lev, across)
    crossing.start()
    for way in range(2):
        if steps[way]:
            ring(way, 0, 1, False).start()

    load.wait()
    for group in range(3):
        regroup_tokens(group, n_lev, token_rows, floats, outgoing)
        if group == 0:
            crossed.wait_recv()
            for way in range(2):
                if steps[way]:
                    ring(way, 1, 1, False).start()
            to_sibling(across).start()
    own = pltpu.make_async_copy(outgoing.at[lev], arrived.at[lev], own_sem)
    own.start()

    def tokens(step, arriving):
        peer = lax.rem(lev + (n_lev - step if arriving else step), n_lev)
        return pltpu.make_async_remote_copy(
            src_ref=outgoing.at[peer],
            dst_ref=arrived.at[peer if arriving else lev],
            send_sem=tok_send.at[step],
            recv_sem=tok_recv.at[step],
            device_id={"lev": peer, "lat": lat},
            device_id_type=MESH,
        )

    for step in range(1, n_lev):
        tokens(step, False).start()

    for step in range(1, steps[0] + 1):
        for stream in range(2):
            for way in range(2):
                if step > steps[way]:
                    continue
                ring(way, stream, step, True).wait_recv()
                if step < steps[way]:
                    ring(way, stream, step + 1, False).start()
                to_sibling(shard_at(stream, -step if way == 0 else step)).start()

    own.wait()
    for step in range(1, n_lev):
        tokens(step, True).wait_recv()
    for step in range(depth):
        for stream in range(2):
            if step or stream:
                from_sibling(shard_at(stream, step)).wait_recv()

    def one_group(g, carry):
        project_levels(g, arrived, gathered, scores, values)
        return carry

    lax.fori_loop(0, n_lev // 4, one_group, 0)
    level_attention(scores, probs, values, attn)
    make_latents(attn, base_ref, gathered, latents)

    half = PATCHES // 2
    edge_out[...] = latents[:, 0:48, :].astype(BF16)
    edge = pltpu.make_async_remote_copy(
        src_ref=edge_out,
        dst_ref=edge_in,
        send_sem=edge_sems.at[0],
        recv_sem=edge_sems.at[1],
        device_id={"lev": lev, "lat": north},
        device_id_type=MESH,
    )
    edge.start()
    for l in range(LATENTS):
        window[l * PATCHES : l * PATCHES + half] = latents[l, half:PATCHES]
    edge.wait_recv()
    for l in range(LATENTS):
        window[l * PATCHES + half : (l + 1) * PATCHES] = edge_in[l].astype(F32)[0:half]
    window_attention(
        lat == n_lat - 1, window, gain_ref, gathered, packed, mixed, done, out_ref
    )

    edge.wait_send()
    crossing.wait_send()
    for step in range(1, n_lev):
        tokens(step, False).wait_send()
    for way in range(2):
        for step in range(1, steps[way] + 1):
            for stream in range(2):
                ring(way, stream, step, False).wait_send()
    for step in range(depth):
        for stream in range(2):
            if step or stream:
                to_sibling(shard_at(stream, step)).wait_send()


def on_device(tokens, query, base, key_w, value_w, out_w, gain, qkv_w, proj_w):
    n_lev, n_lat = lax.axis_size("lev"), lax.axis_size("lat")
    levels, rows, cols, width = tokens.shape
    token_rows = tokens.reshape(levels * rows, cols, width)
    length = LATENTS * PATCHES
    groups = n_lev // 4
    vmem = pl.BlockSpec(memory_space=pltpu.VMEM)
    dma = pltpu.SemaphoreType.DMA
    return pl.pallas_call(
        functools.partial(kernel, n_lev, n_lat),
        out_shape=jax.ShapeDtypeStruct((LATENTS, rows, cols // n_lev, width), BF16),
        in_specs=[pl.BlockSpec(memory_space=pl.ANY)] + [vmem] * 8,
        out_specs=vmem,
        scratch_shapes=[
            pltpu.VMEM((n_lat, 2, SHARD, C_END), BF16),
            pltpu.VMEM((n_lev, 144, width), BF16),
            pltpu.VMEM((n_lev, 144, width), BF16),
            pltpu.VMEM(token_rows.shape, BF16),
            pltpu.VMEM((4, cols + 8, width), F32),
            pltpu.VMEM((groups, 576, 128), F32),
            pltpu.VMEM((groups, 576, 256), BF16),
            pltpu.VMEM((groups, 576, INNER), BF16),
            pltpu.VMEM((length, INNER), F32),
            pltpu.VMEM((LATENTS, PATCHES, width), F32),
            pltpu.VMEM((LATENTS, 48, width), BF16),
            pltpu.VMEM((LATENTS, 48, width), BF16),
            pltpu.VMEM((length, width), F32),
            pltpu.VMEM((length, 3 * width), BF16),
            pltpu.VMEM((length, width), BF16),
            pltpu.VMEM((length, width), F32),
            dma,
            dma,
            dma((n_lev,)),
            dma((n_lev,)),
            dma((2 * n_lat,)),
            dma((2 * n_lat,)),
            dma((n_lat,)),
            dma((n_lat,)),
            dma((2,)),
            dma((2,)),
        ],
        compiler_params=pltpu.CompilerParams(
            collective_id=0, has_side_effects=True, vmem_limit_bytes=48 * 1024 * 1024
        ),
        cost_estimate=pl.CostEstimate(
            flops=6_000_000_000, bytes_accessed=8_000_000, transcendentals=1_000_000
        ),
    )(token_rows, query, base, key_w, value_w, out_w, gain.reshape(1, width), qkv_w, proj_w)


def solution(mesh):
    placed = (
        P("lev", "lat", None, None),
        P(),
        P(),
        P("lat", None),
        P("lat", None),
        P("lat", None),
        P(),
        P("lat", None),
        P("lat", None),
    )
    return jax.shard_map(
        on_device,
        mesh=mesh,
        in_specs=placed,
        out_specs=P(None, "lat", "lev", None),
        check_vma=False,
    )
```

```python
import functools

import jax
import jax.numpy as jnp
from jax import lax
from jax.experimental import pallas as pl
from jax.experimental.pallas import tpu as pltpu
from jax.sharding import PartitionSpec as P

MESH = pl.DeviceIdType.MESH
F32 = jnp.float32
BF16 = jnp.bfloat16

HEAD_DIM = 64
LHEADS = 16
LATENTS = 3
WIN_R = 6
WIN_C = 12
WIDTH = 512
INNER = 1024
PATCHES = WIN_R * WIN_C
SHARD = 16
THIRDS = 3
PART = PATCHES // THIRDS
GROUPS = PART // 8
C_V, EARLY = 128, 640
C_W, C_P, LATE = 512, 1280, 1536


def dot(a, b):
    return jnp.dot(a, b, preferred_element_type=F32)


def dot_t(a, b):
    return lax.dot_general(a, b, (((1,), (1,)), ((), ())), preferred_element_type=F32)


def iota(shape, dim):
    return lax.broadcasted_iota(jnp.int32, shape, dim)


def columns_of(gathered, half, start, stop):
    parts = [gathered[:, side, half, :, start:stop] for side in range(2)]
    return jnp.concatenate([p.reshape(-1, stop - start) for p in parts], axis=0)


def fold_query(query, key_rows):
    own_head = iota((LHEADS, INNER), 0) == iota((LHEADS, INNER), 1) // HEAD_DIM
    spread = [jnp.where(own_head, query[l : l + 1, :].astype(F32), 0.0) for l in range(LATENTS)]
    spread.append(jnp.zeros((128 - LATENTS * LHEADS, INNER), F32))
    spread = jnp.concatenate(spread, axis=0).astype(BF16)
    folded = dot_t(key_rows[...], spread) * (HEAD_DIM**-0.5)
    high = folded.astype(BF16)
    return high, (folded - high.astype(F32)).astype(BF16)


def regroup_tokens(third, devices, token_rows, floats, outgoing):
    cols = devices * WIN_C
    for k in range(4):
        row = (k // 2) * WIN_R + 2 * third + k % 2
        floats[k, 0:cols] = token_rows[row].astype(F32)
        floats[k, cols : cols + 8] = token_rows[row, 0:16].astype(F32)[0:8]
    for i in range(devices):
        first = i * WIN_C + WIN_C // 2
        cut = [floats[k, first : first + WIN_C] for k in range(4)]
        levels = [
            jnp.concatenate(cut[2 * l : 2 * l + 2], axis=0).reshape(GROUPS, 8, WIDTH)
            for l in range(2)
        ]
        for g in range(GROUPS):
            block = jnp.concatenate([levels[l][g] for l in range(2)], axis=0)
            outgoing[third, i, g] = block.astype(BF16)


def level_attention(third, arrived, early, values, turned, attn):
    devices = arrived.shape[1]
    rows = arrived[third].reshape(devices * 2 * PART, WIDTH)
    folded = jnp.concatenate([columns_of(early, c, 0, C_V) for c in range(2)], axis=1)
    both = dot(rows, folded)
    for c in range(2):
        found = dot(rows, columns_of(early, c, C_V, EARLY)).astype(BF16)
        values[:, :, :, c * 512 : c * 512 + 512] = found.reshape(devices, GROUPS, 16, 512)
    scores = (both[:, :128] + both[:, 128:]).reshape(devices, GROUPS, 2, 8, 128)
    own_patch = iota((8, 256), 0) == lax.rem(iota((8, 256), 1), 8)
    head_of = iota((8, 256), 1) // HEAD_DIM
    for g in range(GROUPS):
        level = scores[:, g].reshape(2 * devices, 8, 128)
        weights = jnp.exp(level - jnp.max(level, axis=0, keepdims=True))
        weights = weights * (1.0 / jnp.sum(weights, axis=0, keepdims=True))
        turned[g] = weights.reshape(256, 128).T
        for quad in range(LHEADS // 4):
            spread = []
            for l in range(LATENTS):
                for h in range(4):
                    at = l * LHEADS + quad * 4 + h
                    row = jnp.broadcast_to(turned[g, at : at + 1, :], (8, 256))
                    spread.append(jnp.where(own_patch, row, 0.0))
            spread = jnp.concatenate(spread, axis=0).astype(BF16)
            v = values[:, g, :, quad * 256 : quad * 256 + 256].reshape(256, 256)
            sums = dot(spread, v).reshape(LATENTS, 4, 8, 256)
            for l in range(LATENTS):
                own = jnp.zeros((8, 256), F32)
                for h in range(4):
                    own = jnp.where(head_of == h, sums[l, h], own)
                attn[third, l, g * 8 : g * 8 + 8, quad * 256 : quad * 256 + 256] = own


def make_latents(thirds, attn, base, late, latents):
    parts = [late[:, side, :, :, 0:C_W].reshape(INNER // 2, WIDTH) for side in range(2)]
    weight = jnp.concatenate(parts, axis=0)
    count = len(thirds) * LATENTS
    rows = attn[thirds[0] : thirds[-1] + 1].reshape(count * PART, INNER).astype(BF16)
    mixed = dot(rows, weight).reshape(count, PART, WIDTH)
    for k, third in enumerate(thirds):
        for l in range(LATENTS):
            row = mixed[k * LATENTS + l] + base[l : l + 1, :].astype(F32)
            latents[l, third * PART : (third + 1) * PART] = row.astype(BF16).astype(F32)


def window_attention(last, window, gain, late, packed, mixed, done, out_ref):
    length = LATENTS * PATCHES
    x = window[...]
    center = jnp.mean(x, axis=-1, keepdims=True)
    moved = x - center
    spread = jnp.mean(moved * moved, axis=-1, keepdims=True)
    normed = (moved * lax.rsqrt(spread + 1e-05) * gain[...]).astype(BF16)
    for c in range(2):
        weight = columns_of(late, c, C_W, C_P)
        packed[:, c * 768 : c * 768 + 768] = dot(normed, weight).astype(BF16)
    half = PATCHES // 2

    def region(dim):
        return lax.rem(iota((length, length), dim), PATCHES) >= half

    apart = jnp.logical_and(region(0) != region(1), last)
    bias = jnp.where(apart, -1e30, 0.0)
    first = iota((length, 128), 1) < HEAD_DIM

    for i in range(WIDTH // 128):
        at = i * 128
        q = packed[:, at : at + 128].astype(F32) * (HEAD_DIM**-0.5)
        k = packed[:, WIDTH + at : WIDTH + at + 128]
        v = packed[:, 2 * WIDTH + at : 2 * WIDTH + at + 128]
        outs = []
        for side in (first, jnp.logical_not(first)):
            s = dot_t(jnp.where(side, q, 0.0).astype(BF16), k) + bias
            w = jnp.exp(s - jnp.max(s, axis=-1, keepdims=True))
            w = (w * (1.0 / jnp.sum(w, axis=-1, keepdims=True))).astype(BF16)
            outs.append(dot(w, v))
        mixed[:, at : at + 128] = jnp.where(first, outs[0], outs[1]).astype(BF16)
    for c in range(2):
        weight = columns_of(late, c, C_P, LATE)
        done[:, c * 256 : c * 256 + 256] = x[:, c * 256 : c * 256 + 256] + dot(mixed[...], weight)
    for l in range(LATENTS):
        for r in range(WIN_R):
            at = l * PATCHES + r * WIN_C
            out_ref[l, r] = done[at : at + WIN_C, :].astype(BF16)


def kernel(
    n_lev,
    n_lat,
    tok_hbm,
    q_hbm,
    base_hbm,
    kw_hbm,
    vw_hbm,
    ow_hbm,
    gain_hbm,
    qkvw_hbm,
    pw_hbm,
    out_ref,
    early,
    late,
    arrived,
    outgoing,
    token_rows,
    floats,
    query,
    base,
    key_rows,
    gain,
    values,
    turned,
    attn,
    latents,
    edge_out,
    edge_in,
    window,
    packed,
    mixed,
    done,
    load_sems,
    tok_send,
    tok_recv,
    ring_send,
    ring_recv,
    core_send,
    core_recv,
    hop_send,
    hop_recv,
    edge_sems,
):
    lev, lat = lax.axis_index("lev"), lax.axis_index("lat")
    depth = n_lat // 2
    side, z = lax.div(lat, depth), lax.rem(lat, depth)
    moves = [(q_hbm, query), (kw_hbm, key_rows), (base_hbm, base), (gain_hbm, gain)]
    for c in range(2):
        moves += [
            (vw_hbm.at[:, c * 512 : c * 512 + 512], early.at[z, side, c, :, C_V:EARLY]),
            (ow_hbm.at[c * 16 : c * 16 + 16], late.at[z, side, c, :, 0:C_W]),
            (qkvw_hbm.at[:, c * 768 : c * 768 + 768], late.at[z, side, c, :, C_W:C_P]),
            (pw_hbm.at[:, c * 256 : c * 256 + 256], late.at[z, side, c, :, C_P:LATE]),
        ]
    few = len(moves)
    for third in range(THIRDS):
        for l in range(2):
            rows = pl.ds(l * WIN_R + 2 * third, 2)
            moves.append((tok_hbm.at[rows], token_rows.at[rows]))
    loads = [pltpu.make_async_copy(*m, load_sems.at[i]) for i, m in enumerate(moves)]
    for load in loads:
        load.start()

    core = lax.rem(lev, 2)
    sibling = lev + 1 - 2 * core

    def at_z(step):
        return lax.rem(z + step + depth, depth)

    up, down = side * depth + at_z(1), side * depth + at_z(-1)
    across = (1 - side) * depth + z
    north, south = lax.rem(lat + n_lat - 1, n_lat), lax.rem(lat + 1, n_lat)

    barrier = pltpu.get_barrier_semaphore()
    for peer in (up, down, across, north, south):
        pl.semaphore_signal(
            barrier, inc=1, device_id={"lev": lev, "lat": peer}, device_id_type=MESH
        )
    for k in range(1, n_lev):
        peer = lax.rem(lev + k, n_lev)
        pl.semaphore_signal(
            barrier, inc=1, device_id={"lev": peer, "lat": lat}, device_id_type=MESH
        )
    for load in loads[:few]:
        load.wait()
    folded = fold_query(query, key_rows)
    for c in range(2):
        early[z, side, c, :, 0:C_V] = folded[c]

    def regroup(third):
        loads[few + 2 * third].wait()
        loads[few + 2 * third + 1].wait()
        regroup_tokens(third, n_lev, token_rows, floats, outgoing)

    regroup(0)
    pl.semaphore_wait(barrier, 5 + n_lev - 1)

    gathers = (early, late)
    steps = depth // 2
    way = 1 - 2 * core
    onward = side * depth + at_z(way)

    chunks = [(which, stream) for stream in range(2) for which in range(2)]

    def piece(chunk, at):
        which, stream = chunk
        return gathers[which].at[at, side if stream == 0 else 1 - side]

    def ring(chunk, step, arriving):
        at = at_z(-way * (step if arriving else step - 1))
        where = chunk[0] * 2 + chunk[1]
        return pltpu.make_async_remote_copy(
            src_ref=piece(chunk, at),
            dst_ref=piece(chunk, at),
            send_sem=ring_send.at[where, step],
            recv_sem=ring_recv.at[where, step],
            device_id={"lev": lev, "lat": onward},
            device_id_type=MESH,
        )

    def exchange(chunk, step, arriving):
        at = at_z(way * step if arriving else -way * step)
        where = chunk[0] * 2 + chunk[1]
        return pltpu.make_async_remote_copy(
            src_ref=piece(chunk, at),
            dst_ref=piece(chunk, at),
            send_sem=core_send.at[where, step],
            recv_sem=core_recv.at[where, step],
            device_id={"lev": sibling, "lat": lat},
            device_id_type=MESH,
        )

    def cross(which, arriving):
        at = 1 - side if arriving else side
        return pltpu.make_async_remote_copy(
            src_ref=gathers[which].at[z, at],
            dst_ref=gathers[which].at[z, at],
            send_sem=hop_send.at[which],
            recv_sem=hop_recv.at[which],
            device_id={"lev": lev, "lat": across},
            device_id_type=MESH,
        )

    def tick(step):
        for chunk in chunks:
            ring(chunk, step, True).wait_recv()
            if step < steps:
                ring(chunk, step + 1, False).start()
                exchange(chunk, step, False).start()

    def tokens(third, step, arriving):
        peer = lax.rem(lev + (n_lev - step if arriving else step), n_lev)
        return pltpu.make_async_remote_copy(
            src_ref=outgoing.at[third, peer],
            dst_ref=arrived.at[third, peer if arriving else lev],
            send_sem=tok_send.at[third, step],
            recv_sem=tok_recv.at[third, step],
            device_id={"lev": peer, "lat": lat},
            device_id_type=MESH,
        )

    def own(third):
        return pltpu.make_async_copy(
            outgoing.at[third, lev], arrived.at[third, lev], tok_send.at[third, 0]
        )

    def send_tokens(third):
        for step in range(1, n_lev):
            tokens(third, step, False).start()
        own(third).start()

    def tokens_here(third):
        own(third).wait()
        for step in range(1, n_lev):
            tokens(third, step, True).wait_recv()

    for which in range(2):
        cross(which, False).start()
    for which in range(2):
        ring((which, 0), 1, False).start()
    send_tokens(0)
    regroup(1)
    send_tokens(1)
    for which in range(2):
        cross(which, True).wait_recv()
        ring((which, 1), 1, False).start()
    tick(1)
    regroup(2)
    send_tokens(2)
    for step in range(2, steps + 1):
        tick(step)
    for step in range(1, steps):
        for chunk in chunks:
            exchange(chunk, step, True).wait_recv()

    for third in range(THIRDS):
        tokens_here(third)
        level_attention(third, arrived, early, values, turned, attn)
        if third == 1:
            make_latents((0, 1), attn, base, late, latents)
            edge_out[...] = latents[:, 0:48, :].astype(BF16)
            edge = pltpu.make_async_remote_copy(
                src_ref=edge_out,
                dst_ref=edge_in,
                send_sem=edge_sems.at[0],
                recv_sem=edge_sems.at[1],
                device_id={"lev": lev, "lat": north},
                device_id_type=MESH,
            )
            edge.start()
    make_latents((2,), attn, base, late, latents)

    half = PATCHES // 2
    for l in range(LATENTS):
        window[l * PATCHES : l * PATCHES + half] = latents[l, half:PATCHES]
    edge.wait_recv()
    for l in range(LATENTS):
        window[l * PATCHES + half : (l + 1) * PATCHES] = edge_in[l].astype(F32)[0:half]
    window_attention(lat == n_lat - 1, window, gain, late, packed, mixed, done, out_ref)

    edge.wait_send()
    for third in range(THIRDS):
        for step in range(1, n_lev):
            tokens(third, step, False).wait_send()
    for which in range(2):
        cross(which, False).wait_send()
    for chunk in chunks:
        for step in range(1, steps + 1):
            ring(chunk, step, False).wait_send()
        for step in range(1, steps):
            exchange(chunk, step, False).wait_send()


def on_device(tokens, query, base, key_w, value_w, out_w, gain, qkv_w, proj_w):
    n_lev, n_lat = lax.axis_size("lev"), lax.axis_size("lat")
    levels, rows, cols, width = tokens.shape
    token_rows = tokens.reshape(levels * rows, cols, width)
    gain_row = gain.reshape(1, width)
    length = LATENTS * PATCHES
    dma = pltpu.SemaphoreType.DMA
    return pl.pallas_call(
        functools.partial(kernel, n_lev, n_lat),
        out_shape=jax.ShapeDtypeStruct((LATENTS, rows, cols // n_lev, width), BF16),
        in_specs=[pl.BlockSpec(memory_space=pltpu.HBM)] * 9,
        out_specs=pl.BlockSpec(memory_space=pltpu.VMEM),
        scratch_shapes=[
            pltpu.VMEM((n_lat // 2, 2, 2, SHARD, EARLY), BF16),
            pltpu.VMEM((n_lat // 2, 2, 2, SHARD, LATE), BF16),
            pltpu.VMEM((THIRDS, n_lev, GROUPS, 16, width), BF16),
            pltpu.VMEM((THIRDS, n_lev, GROUPS, 16, width), BF16),
            pltpu.VMEM(token_rows.shape, BF16),
            pltpu.VMEM((4, cols + 8, width), F32),
            pltpu.VMEM(query.shape, BF16),
            pltpu.VMEM(base.shape, BF16),
            pltpu.VMEM(key_w.shape, BF16),
            pltpu.VMEM(gain_row.shape, F32),
            pltpu.VMEM((n_lev, GROUPS, 16, INNER), BF16),
            pltpu.VMEM((GROUPS, 128, 256), F32),
            pltpu.VMEM((THIRDS, LATENTS, PART, INNER), F32),
            pltpu.VMEM((LATENTS, PATCHES, width), F32),
            pltpu.VMEM((LATENTS, 48, width), BF16),
            pltpu.VMEM((LATENTS, 48, width), BF16),
            pltpu.VMEM((length, width), F32),
            pltpu.VMEM((length, 3 * width), BF16),
            pltpu.VMEM((length, width), BF16),
            pltpu.VMEM((length, width), F32),
            dma((12 + 2 * THIRDS,)),
            dma((THIRDS, n_lev)),
            dma((THIRDS, n_lev)),
            dma((4, n_lat // 4 + 1)),
            dma((4, n_lat // 4 + 1)),
            dma((4, n_lat // 4)),
            dma((4, n_lat // 4)),
            dma((2,)),
            dma((2,)),
            dma((2,)),
        ],
        compiler_params=pltpu.CompilerParams(
            collective_id=0, has_side_effects=True, vmem_limit_bytes=62 * 1024 * 1024
        ),
        cost_estimate=pl.CostEstimate(
            flops=6_000_000_000, bytes_accessed=8_000_000, transcendentals=1_000_000
        ),
    )(token_rows, query, base, key_w, value_w, out_w, gain_row, qkv_w, proj_w)


def solution(mesh):
    placed = (
        P("lev", "lat", None, None),
        P(),
        P(),
        P("lat", None),
        P("lat", None),
        P("lat", None),
        P(),
        P("lat", None),
        P("lat", None),
    )
    return jax.shard_map(
        on_device,
        mesh=mesh,
        in_specs=placed,
        out_specs=P(None, "lat", "lev", None),
        check_vma=False,
    )
```

```python
import functools

import jax
import jax.numpy as jnp
from jax import lax
from jax.experimental import pallas as pl
from jax.experimental.pallas import tpu as pltpu
from jax.sharding import PartitionSpec as P

MESH = pl.DeviceIdType.MESH
F32 = jnp.float32
BF16 = jnp.bfloat16

HEAD_DIM = 64
LHEADS = 16
LATENTS = 3
WIN_R = 6
WIN_C = 12
WIDTH = 512
INNER = 1024
PATCHES = WIN_R * WIN_C
SHARD = 16
THIRDS = 3
PART = PATCHES // THIRDS
GROUPS = PART // 8
C_V, EARLY = 128, 1152
C_P, C_O, LATE = 1536, 2048, 3072


def dot(a, b):
    return jnp.dot(a, b, preferred_element_type=F32)


def dot_t(a, b):
    return lax.dot_general(a, b, (((1,), (1,)), ((), ())), preferred_element_type=F32)


def iota(shape, dim):
    return lax.broadcasted_iota(jnp.int32, shape, dim)


def columns_of(gathered, start, stop):
    parts = [gathered[:, side, :, start:stop] for side in range(2)]
    return jnp.concatenate([p.reshape(-1, stop - start) for p in parts], axis=0)


def fold_query(query, key_rows):
    own_head = iota((LHEADS, INNER), 0) == iota((LHEADS, INNER), 1) // HEAD_DIM
    spread = [jnp.where(own_head, query[l : l + 1, :].astype(F32), 0.0) for l in range(LATENTS)]
    spread.append(jnp.zeros((64 - LATENTS * LHEADS, INNER), F32))
    spread = jnp.concatenate(spread * 2, axis=0).astype(BF16)
    folded = dot_t(key_rows[...], spread) * (HEAD_DIM**-0.5)
    high = folded.astype(BF16).astype(F32)
    low = folded - high
    return jnp.where(iota(folded.shape, 1) < 64, high, low).astype(BF16)


def regroup_tokens(third, devices, token_rows, floats, outgoing):
    cols = devices * WIN_C
    for k in range(4):
        row = (k // 2) * WIN_R + 2 * third + k % 2
        floats[k, 0:cols] = token_rows[row].astype(F32)
        floats[k, cols : cols + 8] = token_rows[row, 0:16].astype(F32)[0:8]
    for i in range(devices):
        first = i * WIN_C + WIN_C // 2
        cut = [floats[k, first : first + WIN_C] for k in range(4)]
        levels = [
            jnp.concatenate(cut[2 * l : 2 * l + 2], axis=0).reshape(GROUPS, 8, WIDTH)
            for l in range(2)
        ]
        for g in range(GROUPS):
            block = jnp.concatenate([levels[l][g] for l in range(2)], axis=0)
            outgoing[third, i, g] = block.astype(BF16)


def level_attention(third, arrived, early, values, turned, attn):
    devices = arrived.shape[1]
    rows = arrived[third].reshape(devices * 2 * PART, WIDTH)
    both = dot(rows, columns_of(early, 0, C_V))
    for c in range(2):
        found = dot(rows, columns_of(early, C_V + c * 512, C_V + c * 512 + 512)).astype(BF16)
        values[:, :, :, c * 512 : c * 512 + 512] = found.reshape(devices, GROUPS, 16, 512)
    both = both + jnp.concatenate([both[:, 64:], both[:, :64]], axis=1)
    scores = both.reshape(devices, GROUPS, 2, 8, 128)
    own_patch = iota((8, 256), 0) == lax.rem(iota((8, 256), 1), 8)
    head_of = iota((8, 256), 1) // HEAD_DIM
    for g in range(GROUPS):
        level = scores[:, g].reshape(2 * devices, 8, 128)
        weights = jnp.exp(level - jnp.max(level, axis=0, keepdims=True))
        weights = weights * (1.0 / jnp.sum(weights, axis=0, keepdims=True))
        turned[g] = weights.reshape(256, 128).T
        for quad in range(LHEADS // 4):
            spread = []
            for l in range(LATENTS):
                for h in range(4):
                    at = l * LHEADS + quad * 4 + h
                    row = jnp.broadcast_to(turned[g, at : at + 1, :], (8, 256))
                    spread.append(jnp.where(own_patch, row, 0.0))
            spread = jnp.concatenate(spread, axis=0).astype(BF16)
            v = values[:, g, :, quad * 256 : quad * 256 + 256].reshape(256, 256)
            sums = dot(spread, v).reshape(LATENTS, 4, 8, 256)
            for l in range(LATENTS):
                own = jnp.zeros((8, 256), F32)
                for h in range(4):
                    own = jnp.where(head_of == h, sums[l, h], own)
                attn[third, l, g * 8 : g * 8 + 8, quad * 256 : quad * 256 + 256] = own


def make_latents(thirds, attn, base, late, latents):
    parts = []
    for side in range(2):
        halves = [late[:, side, :, C_O + c * 512 : C_O + c * 512 + 512] for c in range(2)]
        parts.append(jnp.stack(halves, axis=1).reshape(INNER // 2, WIDTH))
    weight = jnp.concatenate(parts, axis=0)
    count = len(thirds) * LATENTS
    rows = attn[thirds[0] : thirds[-1] + 1].reshape(count * PART, INNER).astype(BF16)
    mixed = dot(rows, weight).reshape(count, PART, WIDTH)
    for k, third in enumerate(thirds):
        for l in range(LATENTS):
            row = mixed[k * LATENTS + l] + base[l : l + 1, :].astype(F32)
            latents[l, third * PART : (third + 1) * PART] = row.astype(BF16).astype(F32)


def window_attention(last, window, gain, late, packed, mixed, done, out_ref):
    length = LATENTS * PATCHES
    x = window[...]
    center = jnp.mean(x, axis=-1, keepdims=True)
    moved = x - center
    spread = jnp.mean(moved * moved, axis=-1, keepdims=True)
    normed = (moved * lax.rsqrt(spread + 1e-05) * gain[...]).astype(BF16)
    for c in range(2):
        weight = columns_of(late, c * 768, c * 768 + 768)
        packed[:, c * 768 : c * 768 + 768] = dot(normed, weight).astype(BF16)
    half = PATCHES // 2

    def region(dim):
        return lax.rem(iota((length, length), dim), PATCHES) >= half

    apart = jnp.logical_and(region(0) != region(1), last)
    bias = jnp.where(apart, -1e30, 0.0)
    first = iota((length, 128), 1) < HEAD_DIM

    for i in range(WIDTH // 128):
        at = i * 128
        q = packed[:, at : at + 128].astype(F32) * (HEAD_DIM**-0.5)
        k = packed[:, WIDTH + at : WIDTH + at + 128]
        v = packed[:, 2 * WIDTH + at : 2 * WIDTH + at + 128]
        outs = []
        for side in (first, jnp.logical_not(first)):
            s = dot_t(jnp.where(side, q, 0.0).astype(BF16), k) + bias
            w = jnp.exp(s - jnp.max(s, axis=-1, keepdims=True))
            w = (w * (1.0 / jnp.sum(w, axis=-1, keepdims=True))).astype(BF16)
            outs.append(dot(w, v))
        mixed[:, at : at + 128] = jnp.where(first, outs[0], outs[1]).astype(BF16)
    for c in range(2):
        weight = columns_of(late, C_P + c * 256, C_P + c * 256 + 256)
        done[:, c * 256 : c * 256 + 256] = x[:, c * 256 : c * 256 + 256] + dot(mixed[...], weight)
    for l in range(LATENTS):
        for r in range(WIN_R):
            at = l * PATCHES + r * WIN_C
            out_ref[l, r] = done[at : at + WIN_C, :].astype(BF16)


def kernel(
    n_lev,
    n_lat,
    tok_hbm,
    q_hbm,
    base_hbm,
    kw_hbm,
    vw_hbm,
    ow_hbm,
    gain_hbm,
    qkvw_hbm,
    pw_hbm,
    out_ref,
    early,
    late,
    arrived,
    outgoing,
    token_rows,
    floats,
    query,
    base,
    key_rows,
    gain,
    values,
    turned,
    attn,
    latents,
    edge_out,
    edge_in,
    window,
    packed,
    mixed,
    done,
    load_sems,
    tok_send,
    tok_recv,
    ring_send,
    ring_recv,
    core_send,
    core_recv,
    hop_send,
    hop_recv,
    edge_sems,
):
    lev, lat = lax.axis_index("lev"), lax.axis_index("lat")
    depth = n_lat // 2
    side, z = lax.div(lat, depth), lax.rem(lat, depth)
    moves = [(q_hbm, query), (kw_hbm, key_rows), (base_hbm, base), (gain_hbm, gain)]
    moves += [
        (vw_hbm, early.at[z, side, :, C_V:EARLY]),
        (qkvw_hbm, late.at[z, side, :, 0:C_P]),
        (pw_hbm, late.at[z, side, :, C_P:C_O]),
        (ow_hbm.at[0:16], late.at[z, side, :, C_O : C_O + 512]),
        (ow_hbm.at[16:32], late.at[z, side, :, C_O + 512 : LATE]),
    ]
    few = len(moves)
    for third in range(THIRDS):
        for l in range(2):
            rows = pl.ds(l * WIN_R + 2 * third, 2)
            moves.append((tok_hbm.at[rows], token_rows.at[rows]))
    loads = [pltpu.make_async_copy(*m, load_sems.at[i]) for i, m in enumerate(moves)]
    for load in loads:
        load.start()

    core = lax.rem(lev, 2)
    sibling = lev + 1 - 2 * core

    def at_z(step):
        return lax.rem(z + step + depth, depth)

    up, down = side * depth + at_z(1), side * depth + at_z(-1)
    across = (1 - side) * depth + z
    north, south = lax.rem(lat + n_lat - 1, n_lat), lax.rem(lat + 1, n_lat)

    barrier = pltpu.get_barrier_semaphore()
    for peer in (up, down, across, north, south):
        pl.semaphore_signal(
            barrier, inc=1, device_id={"lev": lev, "lat": peer}, device_id_type=MESH
        )
    for k in range(1, n_lev):
        peer = lax.rem(lev + k, n_lev)
        pl.semaphore_signal(
            barrier, inc=1, device_id={"lev": peer, "lat": lat}, device_id_type=MESH
        )
    for load in loads[:few]:
        load.wait()
    early[z, side, :, 0:C_V] = fold_query(query, key_rows)

    def regroup(third):
        loads[few + 2 * third].wait()
        loads[few + 2 * third + 1].wait()
        regroup_tokens(third, n_lev, token_rows, floats, outgoing)

    pl.semaphore_wait(barrier, 5 + n_lev - 1)

    gathers = (early, late)
    steps = depth // 2
    way = 1 - 2 * core
    onward = side * depth + at_z(way)

    def side_of(stream, step):
        if step == steps:
            return side + core * (1 - 2 * side)
        return side if stream == 0 else 1 - side

    def ring(which, stream, step, arriving):
        at = at_z(-way * (step if arriving else step - 1)), side_of(stream, step)
        return pltpu.make_async_remote_copy(
            src_ref=gathers[which].at[at],
            dst_ref=gathers[which].at[at],
            send_sem=ring_send.at[which * 2 + stream, step],
            recv_sem=ring_recv.at[which * 2 + stream, step],
            device_id={"lev": lev, "lat": onward},
            device_id_type=MESH,
        )

    def exchange(which, stream, step, arriving):
        there = side_of(stream, step)
        if arriving and step == steps:
            there = 1 - there
        at = at_z(way * step if arriving else -way * step), there
        return pltpu.make_async_remote_copy(
            src_ref=gathers[which].at[at],
            dst_ref=gathers[which].at[at],
            send_sem=core_send.at[which * 2 + stream, step],
            recv_sem=core_recv.at[which * 2 + stream, step],
            device_id={"lev": sibling, "lat": lat},
            device_id_type=MESH,
        )

    def streams(step):
        return range(1 if step == steps else 2)

    def cross(which, arriving):
        at = 1 - side if arriving else side
        return pltpu.make_async_remote_copy(
            src_ref=gathers[which].at[z, at],
            dst_ref=gathers[which].at[z, at],
            send_sem=hop_send.at[which],
            recv_sem=hop_recv.at[which],
            device_id={"lev": lev, "lat": across},
            device_id_type=MESH,
        )

    def tick(which, step):
        for stream in streams(step):
            ring(which, stream, step, True).wait_recv()
            if step + 1 < steps:
                ring(which, stream, step + 1, False).start()
            exchange(which, stream, step, False).start()
        if step + 1 == steps:
            ring(which, 0, steps, False).start()

    def all_shared(which):
        for step in range(1, steps + 1):
            for stream in streams(step):
                exchange(which, stream, step, True).wait_recv()

    def tokens(third, step, arriving):
        peer = lax.rem(lev + (n_lev - step if arriving else step), n_lev)
        return pltpu.make_async_remote_copy(
            src_ref=outgoing.at[third, peer],
            dst_ref=arrived.at[third, peer if arriving else lev],
            send_sem=tok_send.at[third, step],
            recv_sem=tok_recv.at[third, step],
            device_id={"lev": peer, "lat": lat},
            device_id_type=MESH,
        )

    def own(third):
        return pltpu.make_async_copy(
            outgoing.at[third, lev], arrived.at[third, lev], tok_send.at[third, 0]
        )

    def send_tokens(third):
        for step in range(1, n_lev):
            tokens(third, step, False).start()
        own(third).start()

    def tokens_here(third):
        own(third).wait()
        for step in range(1, n_lev):
            tokens(third, step, True).wait_recv()

    for which in range(2):
        cross(which, False).start()
        ring(which, 0, 1, False).start()
    regroup(0)
    send_tokens(0)
    for which in range(2):
        cross(which, True).wait_recv()
        ring(which, 1, 1, False).start()
    regroup(1)
    send_tokens(1)
    tick(0, 1)
    regroup(2)
    send_tokens(2)
    for step in range(2, steps + 1):
        tick(0, step)
        tick(1, step - 1)
    all_shared(0)

    for third in range(THIRDS):
        tokens_here(third)
        level_attention(third, arrived, early, values, turned, attn)
        if third == 0:
            tick(1, steps)
        if third == 1:
            all_shared(1)
            make_latents((0, 1), attn, base, late, latents)
            edge_out[...] = latents[:, 0:48, :].astype(BF16)
            edge = pltpu.make_async_remote_copy(
                src_ref=edge_out,
                dst_ref=edge_in,
                send_sem=edge_sems.at[0],
                recv_sem=edge_sems.at[1],
                device_id={"lev": lev, "lat": north},
                device_id_type=MESH,
            )
            edge.start()
    make_latents((2,), attn, base, late, latents)

    half = PATCHES // 2
    for l in range(LATENTS):
        window[l * PATCHES : l * PATCHES + half] = latents[l, half:PATCHES]
    edge.wait_recv()
    for l in range(LATENTS):
        window[l * PATCHES + half : (l + 1) * PATCHES] = edge_in[l].astype(F32)[0:half]
    window_attention(lat == n_lat - 1, window, gain, late, packed, mixed, done, out_ref)

    edge.wait_send()
    for third in range(THIRDS):
        for step in range(1, n_lev):
            tokens(third, step, False).wait_send()
    for which in range(2):
        cross(which, False).wait_send()
    for which in range(2):
        for step in range(1, steps + 1):
            for stream in streams(step):
                ring(which, stream, step, False).wait_send()
                exchange(which, stream, step, False).wait_send()


def on_device(tokens, query, base, key_w, value_w, out_w, gain, qkv_w, proj_w):
    n_lev, n_lat = lax.axis_size("lev"), lax.axis_size("lat")
    levels, rows, cols, width = tokens.shape
    token_rows = tokens.reshape(levels * rows, cols, width)
    gain_row = gain.reshape(1, width)
    length = LATENTS * PATCHES
    dma = pltpu.SemaphoreType.DMA
    return pl.pallas_call(
        functools.partial(kernel, n_lev, n_lat),
        out_shape=jax.ShapeDtypeStruct((LATENTS, rows, cols // n_lev, width), BF16),
        in_specs=[pl.BlockSpec(memory_space=pltpu.HBM)] * 9,
        out_specs=pl.BlockSpec(memory_space=pltpu.VMEM),
        scratch_shapes=[
            pltpu.VMEM((n_lat // 2, 2, SHARD, EARLY), BF16),
            pltpu.VMEM((n_lat // 2, 2, SHARD, LATE), BF16),
            pltpu.VMEM((THIRDS, n_lev, GROUPS, 16, width), BF16),
            pltpu.VMEM((THIRDS, n_lev, GROUPS, 16, width), BF16),
            pltpu.VMEM(token_rows.shape, BF16),
            pltpu.VMEM((4, cols + 8, width), F32),
            pltpu.VMEM(query.shape, BF16),
            pltpu.VMEM(base.shape, BF16),
            pltpu.VMEM(key_w.shape, BF16),
            pltpu.VMEM(gain_row.shape, F32),
            pltpu.VMEM((n_lev, GROUPS, 16, INNER), BF16),
            pltpu.VMEM((GROUPS, 128, 256), F32),
            pltpu.VMEM((THIRDS, LATENTS, PART, INNER), F32),
            pltpu.VMEM((LATENTS, PATCHES, width), F32),
            pltpu.VMEM((LATENTS, 48, width), BF16),
            pltpu.VMEM((LATENTS, 48, width), BF16),
            pltpu.VMEM((length, width), F32),
            pltpu.VMEM((length, 3 * width), BF16),
            pltpu.VMEM((length, width), BF16),
            pltpu.VMEM((length, width), F32),
            dma((9 + 2 * THIRDS,)),
            dma((THIRDS, n_lev)),
            dma((THIRDS, n_lev)),
            dma((4, n_lat // 4 + 1)),
            dma((4, n_lat // 4 + 1)),
            dma((4, n_lat // 4 + 1)),
            dma((4, n_lat // 4 + 1)),
            dma((2,)),
            dma((2,)),
            dma((2,)),
        ],
        compiler_params=pltpu.CompilerParams(
            collective_id=0, has_side_effects=True, vmem_limit_bytes=62 * 1024 * 1024
        ),
        cost_estimate=pl.CostEstimate(
            flops=6_000_000_000, bytes_accessed=8_000_000, transcendentals=1_000_000
        ),
    )(token_rows, query, base, key_w, value_w, out_w, gain_row, qkv_w, proj_w)


def solution(mesh):
    placed = (
        P("lev", "lat", None, None),
        P(),
        P(),
        P("lat", None),
        P("lat", None),
        P("lat", None),
        P(),
        P("lat", None),
        P("lat", None),
    )
    return jax.shard_map(
        on_device,
        mesh=mesh,
        in_specs=placed,
        out_specs=P(None, "lat", "lev", None),
        check_vma=False,
    )
```

```python
import functools

import jax
import jax.numpy as jnp
from jax import lax
from jax.experimental import pallas as pl
from jax.experimental.pallas import tpu as pltpu
from jax.sharding import PartitionSpec as P

MESH = pl.DeviceIdType.MESH
F32 = jnp.float32
BF16 = jnp.bfloat16

HEAD_DIM = 64
LHEADS = 16
LATENTS = 3
WIN_R = 6
WIN_C = 12
WIDTH = 512
INNER = 1024
PATCHES = WIN_R * WIN_C
SHARD = 16
THIRDS = 3
PART = PATCHES // THIRDS
GROUPS = PART // 8
C_V, EARLY = 128, 1152
C_P, C_O, LATE = 1536, 2048, 3072


def dot(a, b):
    return jnp.dot(a, b, preferred_element_type=F32)


def dot_t(a, b):
    return lax.dot_general(a, b, (((1,), (1,)), ((), ())), preferred_element_type=F32)


def iota(shape, dim):
    return lax.broadcasted_iota(jnp.int32, shape, dim)


def columns_of(gathered, start, stop):
    parts = [gathered[:, side, :, start:stop] for side in range(2)]
    return jnp.concatenate([p.reshape(-1, stop - start) for p in parts], axis=0)


def fold_query(query, key_rows):
    own_head = iota((LHEADS, INNER), 0) == iota((LHEADS, INNER), 1) // HEAD_DIM
    spread = [jnp.where(own_head, query[l : l + 1, :].astype(F32), 0.0) for l in range(LATENTS)]
    spread.append(jnp.zeros((64 - LATENTS * LHEADS, INNER), F32))
    spread = jnp.concatenate(spread * 2, axis=0).astype(BF16)
    folded = dot_t(key_rows[...], spread) * (HEAD_DIM**-0.5)
    high = folded.astype(BF16).astype(F32)
    low = folded - high
    return jnp.where(iota(folded.shape, 1) < 64, high, low).astype(BF16)


def regroup_tokens(third, devices, token_rows, floats, outgoing):
    cols = devices * WIN_C
    for k in range(4):
        row = (k // 2) * WIN_R + 2 * third + k % 2
        floats[k, 0:cols] = token_rows[row].astype(F32)
        floats[k, cols : cols + 8] = token_rows[row, 0:16].astype(F32)[0:8]
    for i in range(devices):
        first = i * WIN_C + WIN_C // 2
        cut = [floats[k, first : first + WIN_C] for k in range(4)]
        levels = [
            jnp.concatenate(cut[2 * l : 2 * l + 2], axis=0).reshape(GROUPS, 8, WIDTH)
            for l in range(2)
        ]
        for g in range(GROUPS):
            block = jnp.concatenate([levels[l][g] for l in range(2)], axis=0)
            outgoing[third, i, g] = block.astype(BF16)


def level_attention(third, arrived, early, values, turned, attn):
    devices = arrived.shape[1]
    rows = arrived[third].reshape(devices * 2 * PART, WIDTH)
    both = dot(rows, columns_of(early, 0, C_V))
    for c in range(2):
        found = dot(rows, columns_of(early, C_V + c * 512, C_V + c * 512 + 512)).astype(BF16)
        values[:, :, :, c * 512 : c * 512 + 512] = found.reshape(devices, GROUPS, 16, 512)
    both = both + jnp.concatenate([both[:, 64:], both[:, :64]], axis=1)
    scores = both.reshape(devices, GROUPS, 2, 8, 128)
    own_patch = iota((8, 256), 0) == lax.rem(iota((8, 256), 1), 8)
    head_of = iota((8, 256), 1) // HEAD_DIM
    for g in range(GROUPS):
        level = scores[:, g].reshape(2 * devices, 8, 128)
        weights = jnp.exp(level - jnp.max(level, axis=0, keepdims=True))
        weights = weights * (1.0 / jnp.sum(weights, axis=0, keepdims=True))
        turned[g] = weights.reshape(256, 128).T
        for quad in range(LHEADS // 4):
            spread = []
            for l in range(LATENTS):
                for h in range(4):
                    at = l * LHEADS + quad * 4 + h
                    row = jnp.broadcast_to(turned[g, at : at + 1, :], (8, 256))
                    spread.append(jnp.where(own_patch, row, 0.0))
            spread = jnp.concatenate(spread, axis=0).astype(BF16)
            v = values[:, g, :, quad * 256 : quad * 256 + 256].reshape(256, 256)
            sums = dot(spread, v).reshape(LATENTS, 4, 8, 256)
            for l in range(LATENTS):
                own = jnp.zeros((8, 256), F32)
                for h in range(4):
                    own = jnp.where(head_of == h, sums[l, h], own)
                attn[third, l, g * 8 : g * 8 + 8, quad * 256 : quad * 256 + 256] = own


def make_latents(thirds, attn, base, late, latents):
    parts = []
    for side in range(2):
        halves = [late[:, side, :, C_O + c * 512 : C_O + c * 512 + 512] for c in range(2)]
        parts.append(jnp.stack(halves, axis=1).reshape(INNER // 2, WIDTH))
    weight = jnp.concatenate(parts, axis=0)
    count = len(thirds) * LATENTS
    rows = attn[thirds[0] : thirds[-1] + 1].reshape(count * PART, INNER).astype(BF16)
    mixed = dot(rows, weight).reshape(count, PART, WIDTH)
    for k, third in enumerate(thirds):
        for l in range(LATENTS):
            row = mixed[k * LATENTS + l] + base[l : l + 1, :].astype(F32)
            latents[l, third * PART : (third + 1) * PART] = row.astype(BF16).astype(F32)


def window_attention(last, window, gain, late, packed, mixed, done, out_ref):
    length = LATENTS * PATCHES
    x = window[...]
    center = jnp.mean(x, axis=-1, keepdims=True)
    moved = x - center
    spread = jnp.mean(moved * moved, axis=-1, keepdims=True)
    normed = (moved * lax.rsqrt(spread + 1e-05) * gain[...]).astype(BF16)
    for c in range(2):
        weight = columns_of(late, c * 768, c * 768 + 768)
        packed[:, c * 768 : c * 768 + 768] = dot(normed, weight).astype(BF16)
    half = PATCHES // 2

    def region(dim):
        return lax.rem(iota((length, length), dim), PATCHES) >= half

    apart = jnp.logical_and(region(0) != region(1), last)
    bias = jnp.where(apart, -1e30, 0.0)
    first = iota((length, 128), 1) < HEAD_DIM

    for i in range(WIDTH // 128):
        at = i * 128
        q = packed[:, at : at + 128].astype(F32) * (HEAD_DIM**-0.5)
        k = packed[:, WIDTH + at : WIDTH + at + 128]
        v = packed[:, 2 * WIDTH + at : 2 * WIDTH + at + 128]
        outs = []
        for side in (first, jnp.logical_not(first)):
            s = dot_t(jnp.where(side, q, 0.0).astype(BF16), k) + bias
            w = jnp.exp(s - jnp.max(s, axis=-1, keepdims=True))
            w = (w * (1.0 / jnp.sum(w, axis=-1, keepdims=True))).astype(BF16)
            outs.append(dot(w, v))
        mixed[:, at : at + 128] = jnp.where(first, outs[0], outs[1]).astype(BF16)
    for c in range(2):
        weight = columns_of(late, C_P + c * 256, C_P + c * 256 + 256)
        done[:, c * 256 : c * 256 + 256] = x[:, c * 256 : c * 256 + 256] + dot(mixed[...], weight)
    for l in range(LATENTS):
        for r in range(WIN_R):
            at = l * PATCHES + r * WIN_C
            out_ref[l, r] = done[at : at + WIN_C, :].astype(BF16)


def kernel(
    n_lev,
    n_lat,
    tok_hbm,
    q_hbm,
    base_hbm,
    kw_hbm,
    vw_hbm,
    ow_hbm,
    gain_hbm,
    qkvw_hbm,
    pw_hbm,
    out_ref,
    early,
    late,
    arrived,
    outgoing,
    token_rows,
    floats,
    query,
    base,
    key_rows,
    gain,
    values,
    turned,
    attn,
    latents,
    edge_out,
    edge_in,
    window,
    packed,
    mixed,
    done,
    load_sems,
    tok_send,
    tok_recv,
    ring_send,
    ring_recv,
    core_send,
    core_recv,
    hop_send,
    hop_recv,
    edge_sems,
):
    lev, lat = lax.axis_index("lev"), lax.axis_index("lat")
    depth = n_lat // 2
    side, z = lax.div(lat, depth), lax.rem(lat, depth)
    moves = []
    for third in range(THIRDS):
        for l in range(2):
            rows = pl.ds(l * WIN_R + 2 * third, 2)
            moves.append((tok_hbm.at[rows], token_rows.at[rows]))
    moves += [(q_hbm, query), (kw_hbm, key_rows), (base_hbm, base), (gain_hbm, gain)]
    moves += [
        (vw_hbm, early.at[z, side, :, C_V:EARLY]),
        (qkvw_hbm, late.at[z, side, :, 0:C_P]),
        (pw_hbm, late.at[z, side, :, C_P:C_O]),
        (ow_hbm.at[0:16], late.at[z, side, :, C_O : C_O + 512]),
        (ow_hbm.at[16:32], late.at[z, side, :, C_O + 512 : LATE]),
    ]
    loads = [pltpu.make_async_copy(*m, load_sems.at[i]) for i, m in enumerate(moves)]
    first = loads[:2] + loads[2 * THIRDS :]
    for load in first + loads[2 : 2 * THIRDS]:
        load.start()

    core = lax.rem(lev, 2)
    sibling = lev + 1 - 2 * core

    def at_z(step):
        return lax.rem(z + step + depth, depth)

    up, down = side * depth + at_z(1), side * depth + at_z(-1)
    across = (1 - side) * depth + z
    north, south = lax.rem(lat + n_lat - 1, n_lat), lax.rem(lat + 1, n_lat)

    barrier = pltpu.get_barrier_semaphore()
    for peer in (up, down, across, north, south):
        pl.semaphore_signal(
            barrier, inc=1, device_id={"lev": lev, "lat": peer}, device_id_type=MESH
        )
    for k in range(1, n_lev):
        peer = lax.rem(lev + k, n_lev)
        pl.semaphore_signal(
            barrier, inc=1, device_id={"lev": peer, "lat": lat}, device_id_type=MESH
        )

    def regroup(third):
        loads[2 * third].wait()
        loads[2 * third + 1].wait()
        regroup_tokens(third, n_lev, token_rows, floats, outgoing)

    regroup(0)
    for load in first[2:]:
        load.wait()
    early[z, side, :, 0:C_V] = fold_query(query, key_rows)
    pl.semaphore_wait(barrier, 5 + n_lev - 1)

    gathers = (early, late)
    steps = depth // 2
    way = 1 - 2 * core
    onward = side * depth + at_z(way)

    def side_of(stream, step):
        if step == steps:
            return side + core * (1 - 2 * side)
        return side if stream == 0 else 1 - side

    def ring(which, stream, step, arriving):
        at = at_z(-way * (step if arriving else step - 1)), side_of(stream, step)
        return pltpu.make_async_remote_copy(
            src_ref=gathers[which].at[at],
            dst_ref=gathers[which].at[at],
            send_sem=ring_send.at[which * 2 + stream, step],
            recv_sem=ring_recv.at[which * 2 + stream, step],
            device_id={"lev": lev, "lat": onward},
            device_id_type=MESH,
        )

    def exchange(which, stream, step, arriving):
        there = side_of(stream, step)
        if arriving and step == steps:
            there = 1 - there
        at = at_z(way * step if arriving else -way * step), there
        return pltpu.make_async_remote_copy(
            src_ref=gathers[which].at[at],
            dst_ref=gathers[which].at[at],
            send_sem=core_send.at[which * 2 + stream, step],
            recv_sem=core_recv.at[which * 2 + stream, step],
            device_id={"lev": sibling, "lat": lat},
            device_id_type=MESH,
        )

    def streams(step):
        return range(1 if step == steps else 2)

    def cross(which, arriving):
        at = 1 - side if arriving else side
        return pltpu.make_async_remote_copy(
            src_ref=gathers[which].at[z, at],
            dst_ref=gathers[which].at[z, at],
            send_sem=hop_send.at[which],
            recv_sem=hop_recv.at[which],
            device_id={"lev": lev, "lat": across},
            device_id_type=MESH,
        )

    def tick(which, step):
        for stream in streams(step):
            ring(which, stream, step, True).wait_recv()
            if step + 1 < steps:
                ring(which, stream, step + 1, False).start()
            exchange(which, stream, step, False).start()
        if step + 1 == steps:
            ring(which, 0, steps, False).start()

    def all_shared(which):
        for step in range(1, steps + 1):
            for stream in streams(step):
                exchange(which, stream, step, True).wait_recv()

    def tokens(third, step, arriving):
        peer = lax.rem(lev + (n_lev - step if arriving else step), n_lev)
        return pltpu.make_async_remote_copy(
            src_ref=outgoing.at[third, peer],
            dst_ref=arrived.at[third, peer if arriving else lev],
            send_sem=tok_send.at[third, step],
            recv_sem=tok_recv.at[third, step],
            device_id={"lev": peer, "lat": lat},
            device_id_type=MESH,
        )

    def own(third):
        return pltpu.make_async_copy(
            outgoing.at[third, lev], arrived.at[third, lev], tok_send.at[third, 0]
        )

    def send_tokens(third):
        for step in range(1, n_lev):
            tokens(third, step, False).start()
        own(third).start()

    def tokens_here(third):
        own(third).wait()
        for step in range(1, n_lev):
            tokens(third, step, True).wait_recv()

    for which in range(2):
        cross(which, False).start()
        ring(which, 0, 1, False).start()
    send_tokens(0)
    for which in range(2):
        cross(which, True).wait_recv()
        ring(which, 1, 1, False).start()
    regroup(1)
    send_tokens(1)
    tick(0, 1)
    regroup(2)
    send_tokens(2)
    for step in range(2, steps + 1):
        tick(0, step)
        tick(1, step - 1)
    all_shared(0)

    for third in range(THIRDS):
        tokens_here(third)
        level_attention(third, arrived, early, values, turned, attn)
        if third == 0:
            tick(1, steps)
        if third == 1:
            all_shared(1)
            make_latents((0, 1), attn, base, late, latents)
            edge_out[...] = latents[:, 0:48, :].astype(BF16)
            edge = pltpu.make_async_remote_copy(
                src_ref=edge_out,
                dst_ref=edge_in,
                send_sem=edge_sems.at[0],
                recv_sem=edge_sems.at[1],
                device_id={"lev": lev, "lat": north},
                device_id_type=MESH,
            )
            edge.start()
    make_latents((2,), attn, base, late, latents)

    half = PATCHES // 2
    for l in range(LATENTS):
        window[l * PATCHES : l * PATCHES + half] = latents[l, half:PATCHES]
    edge.wait_recv()
    for l in range(LATENTS):
        window[l * PATCHES + half : (l + 1) * PATCHES] = edge_in[l].astype(F32)[0:half]
    window_attention(lat == n_lat - 1, window, gain, late, packed, mixed, done, out_ref)

    edge.wait_send()
    for third in range(THIRDS):
        for step in range(1, n_lev):
            tokens(third, step, False).wait_send()
    for which in range(2):
        cross(which, False).wait_send()
    for which in range(2):
        for step in range(1, steps + 1):
            for stream in streams(step):
                ring(which, stream, step, False).wait_send()
                exchange(which, stream, step, False).wait_send()


def on_device(tokens, query, base, key_w, value_w, out_w, gain, qkv_w, proj_w):
    n_lev, n_lat = lax.axis_size("lev"), lax.axis_size("lat")
    levels, rows, cols, width = tokens.shape
    token_rows = tokens.reshape(levels * rows, cols, width)
    gain_row = gain.reshape(1, width)
    operands = [
        pltpu.with_memory_space_constraint(operand, pltpu.HBM)
        for operand in (token_rows, query, base, key_w, value_w, out_w, gain_row, qkv_w, proj_w)
    ]
    length = LATENTS * PATCHES
    dma = pltpu.SemaphoreType.DMA
    return pl.pallas_call(
        functools.partial(kernel, n_lev, n_lat),
        out_shape=jax.ShapeDtypeStruct((LATENTS, rows, cols // n_lev, width), BF16),
        in_specs=[pl.BlockSpec(memory_space=pltpu.HBM)] * 9,
        out_specs=pl.BlockSpec(memory_space=pltpu.VMEM),
        scratch_shapes=[
            pltpu.VMEM((n_lat // 2, 2, SHARD, EARLY), BF16),
            pltpu.VMEM((n_lat // 2, 2, SHARD, LATE), BF16),
            pltpu.VMEM((THIRDS, n_lev, GROUPS, 16, width), BF16),
            pltpu.VMEM((THIRDS, n_lev, GROUPS, 16, width), BF16),
            pltpu.VMEM(token_rows.shape, BF16),
            pltpu.VMEM((4, cols + 8, width), F32),
            pltpu.VMEM(query.shape, BF16),
            pltpu.VMEM(base.shape, BF16),
            pltpu.VMEM(key_w.shape, BF16),
            pltpu.VMEM(gain_row.shape, F32),
            pltpu.VMEM((n_lev, GROUPS, 16, INNER), BF16),
            pltpu.VMEM((GROUPS, 128, 256), F32),
            pltpu.VMEM((THIRDS, LATENTS, PART, INNER), F32),
            pltpu.VMEM((LATENTS, PATCHES, width), F32),
            pltpu.VMEM((LATENTS, 48, width), BF16),
            pltpu.VMEM((LATENTS, 48, width), BF16),
            pltpu.VMEM((length, width), F32),
            pltpu.VMEM((length, 3 * width), BF16),
            pltpu.VMEM((length, width), BF16),
            pltpu.VMEM((length, width), F32),
            dma((9 + 2 * THIRDS,)),
            dma((THIRDS, n_lev)),
            dma((THIRDS, n_lev)),
            dma((4, n_lat // 4 + 1)),
            dma((4, n_lat // 4 + 1)),
            dma((4, n_lat // 4 + 1)),
            dma((4, n_lat // 4 + 1)),
            dma((2,)),
            dma((2,)),
            dma((2,)),
        ],
        compiler_params=pltpu.CompilerParams(
            collective_id=0, has_side_effects=True, vmem_limit_bytes=44 * 1024 * 1024
        ),
        cost_estimate=pl.CostEstimate(
            flops=6_000_000_000, bytes_accessed=8_000_000, transcendentals=1_000_000
        ),
    )(*operands)


def solution(mesh):
    placed = (
        P("lev", "lat", None, None),
        P(),
        P(),
        P("lat", None),
        P("lat", None),
        P("lat", None),
        P(),
        P("lat", None),
        P("lat", None),
    )
    return jax.shard_map(
        on_device,
        mesh=mesh,
        in_specs=placed,
        out_specs=P(None, "lat", "lev", None),
        check_vma=False,
    )
```

```python
import functools

import jax
import jax.numpy as jnp
from jax import lax
from jax.experimental import pallas as pl
from jax.experimental.pallas import tpu as pltpu
from jax.sharding import PartitionSpec as P

MESH = pl.DeviceIdType.MESH
F32 = jnp.float32
BF16 = jnp.bfloat16

HEAD_DIM = 64
LHEADS = 16
LATENTS = 3
WIN_R = 6
WIN_C = 12
WIDTH = 512
INNER = 1024
PATCHES = WIN_R * WIN_C
SHARD = 16
THIRDS = 3
PART = PATCHES // THIRDS
GROUPS = PART // 8
C_V, EARLY = 128, 1152
C_P, C_O, LATE = 1536, 2048, 3072


def dot(a, b):
    return jnp.dot(a, b, preferred_element_type=F32)


def dot_t(a, b):
    return lax.dot_general(a, b, (((1,), (1,)), ((), ())), preferred_element_type=F32)


def iota(shape, dim):
    return lax.broadcasted_iota(jnp.int32, shape, dim)


def columns_of(gathered, start, stop):
    parts = [gathered[:, side, :, start:stop] for side in range(2)]
    return jnp.concatenate([p.reshape(-1, stop - start) for p in parts], axis=0)


def fold_query(query, key_rows):
    own_head = iota((LHEADS, INNER), 0) == iota((LHEADS, INNER), 1) // HEAD_DIM
    spread = [jnp.where(own_head, query[l : l + 1, :].astype(F32), 0.0) for l in range(LATENTS)]
    spread.append(jnp.zeros((64 - LATENTS * LHEADS, INNER), F32))
    spread = jnp.concatenate(spread * 2, axis=0).astype(BF16)
    folded = dot_t(key_rows[...], spread) * (HEAD_DIM**-0.5)
    high = folded.astype(BF16).astype(F32)
    low = folded - high
    return jnp.where(iota(folded.shape, 1) < 64, high, low).astype(BF16)


def regroup_tokens(third, devices, token_rows, floats, outgoing):
    cols = devices * WIN_C
    for k in range(4):
        row = (k // 2) * WIN_R + 2 * third + k % 2
        floats[k, 0:cols] = token_rows[row].astype(F32)
        floats[k, cols : cols + 8] = token_rows[row, 0:16].astype(F32)[0:8]
    for i in range(devices):
        first = i * WIN_C + WIN_C // 2
        cut = [floats[k, first : first + WIN_C] for k in range(4)]
        levels = [
            jnp.concatenate(cut[2 * l : 2 * l + 2], axis=0).reshape(GROUPS, 8, WIDTH)
            for l in range(2)
        ]
        for g in range(GROUPS):
            block = jnp.concatenate([levels[l][g] for l in range(2)], axis=0)
            outgoing[third, i, g] = block.astype(BF16)


def level_attention(third, arrived, early, values, turned, attn):
    devices = arrived.shape[1]
    rows = arrived[third].reshape(devices * 2 * PART, WIDTH)
    both = dot(rows, columns_of(early, 0, C_V))
    for c in range(2):
        found = dot(rows, columns_of(early, C_V + c * 512, C_V + c * 512 + 512)).astype(BF16)
        values[:, :, :, c * 512 : c * 512 + 512] = found.reshape(devices, GROUPS, 16, 512)
    both = both + jnp.concatenate([both[:, 64:], both[:, :64]], axis=1)
    scores = both.reshape(devices, GROUPS, 2, 8, 128)
    own_patch = iota((8, 256), 0) == lax.rem(iota((8, 256), 1), 8)
    head_of = iota((8, 256), 1) // HEAD_DIM
    for g in range(GROUPS):
        level = scores[:, g].reshape(2 * devices, 8, 128)
        weights = jnp.exp(level - jnp.max(level, axis=0, keepdims=True))
        weights = weights * (1.0 / jnp.sum(weights, axis=0, keepdims=True))
        turned[g] = weights.reshape(256, 128).T
        for quad in range(LHEADS // 4):
            spread = []
            for l in range(LATENTS):
                for h in range(4):
                    at = l * LHEADS + quad * 4 + h
                    row = jnp.broadcast_to(turned[g, at : at + 1, :], (8, 256))
                    spread.append(jnp.where(own_patch, row, 0.0))
            spread = jnp.concatenate(spread, axis=0).astype(BF16)
            v = values[:, g, :, quad * 256 : quad * 256 + 256].reshape(256, 256)
            sums = dot(spread, v).reshape(LATENTS, 4, 8, 256)
            for l in range(LATENTS):
                own = jnp.zeros((8, 256), F32)
                for h in range(4):
                    own = jnp.where(head_of == h, sums[l, h], own)
                attn[third, l, g * 8 : g * 8 + 8, quad * 256 : quad * 256 + 256] = own


def make_latents(thirds, attn, base, late, latents):
    parts = []
    for side in range(2):
        halves = [late[:, side, :, C_O + c * 512 : C_O + c * 512 + 512] for c in range(2)]
        parts.append(jnp.stack(halves, axis=1).reshape(INNER // 2, WIDTH))
    weight = jnp.concatenate(parts, axis=0)
    count = len(thirds) * LATENTS
    rows = attn[thirds[0] : thirds[-1] + 1].reshape(count * PART, INNER).astype(BF16)
    mixed = dot(rows, weight).reshape(count, PART, WIDTH)
    for k, third in enumerate(thirds):
        for l in range(LATENTS):
            row = mixed[k * LATENTS + l] + base[l : l + 1, :].astype(F32)
            latents[l, third * PART : (third + 1) * PART] = row.astype(BF16).astype(F32)


def window_attention(last, window, gain, late, packed, mixed, done, out_ref):
    length = LATENTS * PATCHES
    x = window[...]
    center = jnp.mean(x, axis=-1, keepdims=True)
    moved = x - center
    spread = jnp.mean(moved * moved, axis=-1, keepdims=True)
    normed = (moved * lax.rsqrt(spread + 1e-05) * gain[...]).astype(BF16)
    for c in range(2):
        weight = columns_of(late, c * 768, c * 768 + 768)
        packed[:, c * 768 : c * 768 + 768] = dot(normed, weight).astype(BF16)
    half = PATCHES // 2

    def region(dim):
        return lax.rem(iota((length, length), dim), PATCHES) >= half

    apart = jnp.logical_and(region(0) != region(1), last)
    bias = jnp.where(apart, -1e30, 0.0)
    first = iota((length, 128), 1) < HEAD_DIM

    for i in range(WIDTH // 128):
        at = i * 128
        q = packed[:, at : at + 128].astype(F32) * (HEAD_DIM**-0.5)
        k = packed[:, WIDTH + at : WIDTH + at + 128]
        v = packed[:, 2 * WIDTH + at : 2 * WIDTH + at + 128]
        outs = []
        for side in (first, jnp.logical_not(first)):
            s = dot_t(jnp.where(side, q, 0.0).astype(BF16), k) + bias
            w = jnp.exp(s - jnp.max(s, axis=-1, keepdims=True))
            w = (w * (1.0 / jnp.sum(w, axis=-1, keepdims=True))).astype(BF16)
            outs.append(dot(w, v))
        mixed[:, at : at + 128] = jnp.where(first, outs[0], outs[1]).astype(BF16)
    for c in range(2):
        weight = columns_of(late, C_P + c * 256, C_P + c * 256 + 256)
        done[:, c * 256 : c * 256 + 256] = x[:, c * 256 : c * 256 + 256] + dot(mixed[...], weight)
    for l in range(LATENTS):
        for r in range(WIN_R):
            at = l * PATCHES + r * WIN_C
            out_ref[l, r] = done[at : at + WIN_C, :].astype(BF16)


def kernel(
    n_lev,
    n_lat,
    tok_hbm,
    q_hbm,
    base_hbm,
    kw_hbm,
    vw_hbm,
    ow_hbm,
    gain_hbm,
    qkvw_hbm,
    pw_hbm,
    out_ref,
    early,
    late,
    arrived,
    outgoing,
    token_rows,
    floats,
    query,
    base,
    key_rows,
    gain,
    values,
    turned,
    attn,
    latents,
    edge_out,
    edge_in,
    window,
    packed,
    mixed,
    done,
    load_sems,
    tok_send,
    tok_recv,
    ring_send,
    ring_recv,
    core_send,
    core_recv,
    hop_send,
    hop_recv,
    edge_sems,
):
    lev, lat = lax.axis_index("lev"), lax.axis_index("lat")
    depth = n_lat // 2
    side, z = lax.div(lat, depth), lax.rem(lat, depth)
    moves = []
    for third in range(THIRDS):
        for l in range(2):
            rows = pl.ds(l * WIN_R + 2 * third, 2)
            moves.append((tok_hbm.at[rows], token_rows.at[rows]))
    moves += [(q_hbm, query), (kw_hbm, key_rows), (base_hbm, base), (gain_hbm, gain)]
    moves += [
        (vw_hbm, early.at[z, side, :, C_V:EARLY]),
        (qkvw_hbm, late.at[z, side, :, 0:C_P]),
        (pw_hbm, late.at[z, side, :, C_P:C_O]),
        (ow_hbm.at[0:16], late.at[z, side, :, C_O : C_O + 512]),
        (ow_hbm.at[16:32], late.at[z, side, :, C_O + 512 : LATE]),
    ]
    loads = [pltpu.make_async_copy(*m, load_sems.at[i]) for i, m in enumerate(moves)]
    first = loads[:2] + loads[2 * THIRDS :]
    for load in first + loads[2 : 2 * THIRDS]:
        load.start()

    core = lax.rem(lev, 2)
    sibling = lev + 1 - 2 * core

    def at_z(step):
        return lax.rem(z + step + depth, depth)

    up, down = side * depth + at_z(1), side * depth + at_z(-1)
    across = (1 - side) * depth + z
    north, south = lax.rem(lat + n_lat - 1, n_lat), lax.rem(lat + 1, n_lat)

    barrier = pltpu.get_barrier_semaphore()
    for peer in (up, down, across, north, south):
        pl.semaphore_signal(
            barrier, inc=1, device_id={"lev": lev, "lat": peer}, device_id_type=MESH
        )
    for k in range(1, n_lev):
        peer = lax.rem(lev + k, n_lev)
        pl.semaphore_signal(
            barrier, inc=1, device_id={"lev": peer, "lat": lat}, device_id_type=MESH
        )

    def regroup(third):
        loads[2 * third].wait()
        loads[2 * third + 1].wait()
        regroup_tokens(third, n_lev, token_rows, floats, outgoing)

    regroup(0)
    for load in first[2:]:
        load.wait()
    early[z, side, :, 0:C_V] = fold_query(query, key_rows)
    pl.semaphore_wait(barrier, 5 + n_lev - 1)

    gathers = (early, late)
    steps = depth // 2
    way = 1 - 2 * core
    onward = side * depth + at_z(way)

    def side_of(stream, step):
        if step == steps:
            return side + core * (1 - 2 * side)
        return side if stream == 0 else 1 - side

    def ring(which, stream, step, arriving):
        at = at_z(-way * (step if arriving else step - 1)), side_of(stream, step)
        return pltpu.make_async_remote_copy(
            src_ref=gathers[which].at[at],
            dst_ref=gathers[which].at[at],
            send_sem=ring_send.at[which * 2 + stream, step],
            recv_sem=ring_recv.at[which * 2 + stream, step],
            device_id={"lev": lev, "lat": onward},
            device_id_type=MESH,
        )

    def exchange(which, stream, step, arriving):
        there = side_of(stream, step)
        if arriving and step == steps:
            there = 1 - there
        at = at_z(way * step if arriving else -way * step), there
        return pltpu.make_async_remote_copy(
            src_ref=gathers[which].at[at],
            dst_ref=gathers[which].at[at],
            send_sem=core_send.at[which * 2 + stream, step],
            recv_sem=core_recv.at[which * 2 + stream, step],
            device_id={"lev": sibling, "lat": lat},
            device_id_type=MESH,
        )

    def streams(step):
        return range(1 if step == steps else 2)

    def cross(which, arriving):
        at = 1 - side if arriving else side
        return pltpu.make_async_remote_copy(
            src_ref=gathers[which].at[z, at],
            dst_ref=gathers[which].at[z, at],
            send_sem=hop_send.at[which],
            recv_sem=hop_recv.at[which],
            device_id={"lev": lev, "lat": across},
            device_id_type=MESH,
        )

    def tick(kinds, step):
        for stream in streams(step):
            for which in kinds:
                ring(which, stream, step, True).wait_recv()
                if step + 1 < steps:
                    ring(which, stream, step + 1, False).start()
                elif step < steps and stream == 1:
                    ring(which, 0, steps, False).start()
                exchange(which, stream, step, False).start()

    def all_shared(which):
        for step in range(1, steps + 1):
            for stream in streams(step):
                exchange(which, stream, step, True).wait_recv()

    def tokens(third, step, arriving):
        peer = lax.rem(lev + (n_lev - step if arriving else step), n_lev)
        return pltpu.make_async_remote_copy(
            src_ref=outgoing.at[third, peer],
            dst_ref=arrived.at[third, peer if arriving else lev],
            send_sem=tok_send.at[third, step],
            recv_sem=tok_recv.at[third, step],
            device_id={"lev": peer, "lat": lat},
            device_id_type=MESH,
        )

    def own(third):
        return pltpu.make_async_copy(
            outgoing.at[third, lev], arrived.at[third, lev], tok_send.at[third, 0]
        )

    def send_tokens(third):
        for step in range(1, n_lev):
            tokens(third, step, False).start()
        own(third).start()

    def tokens_here(third):
        own(third).wait()
        for step in range(1, n_lev):
            tokens(third, step, True).wait_recv()

    for which in range(2):
        cross(which, False).start()
        ring(which, 0, 1, False).start()
    send_tokens(0)
    for which in range(2):
        cross(which, True).wait_recv()
        ring(which, 1, 1, False).start()
    regroup(1)
    send_tokens(1)
    tick((0, 1), 1)
    regroup(2)
    send_tokens(2)
    for step in range(2, steps):
        tick((0, 1), step)
    tick((0,), steps)
    all_shared(0)

    for third in range(THIRDS):
        tokens_here(third)
        level_attention(third, arrived, early, values, turned, attn)
        if third == 0:
            tick((1,), steps)
        if third == 1:
            all_shared(1)
            make_latents((0, 1), attn, base, late, latents)
            edge_out[...] = latents[:, 0:48, :].astype(BF16)
            edge = pltpu.make_async_remote_copy(
                src_ref=edge_out,
                dst_ref=edge_in,
                send_sem=edge_sems.at[0],
                recv_sem=edge_sems.at[1],
                device_id={"lev": lev, "lat": north},
                device_id_type=MESH,
            )
            edge.start()
    make_latents((2,), attn, base, late, latents)

    half = PATCHES // 2
    for l in range(LATENTS):
        window[l * PATCHES : l * PATCHES + half] = latents[l, half:PATCHES]
    edge.wait_recv()
    for l in range(LATENTS):
        window[l * PATCHES + half : (l + 1) * PATCHES] = edge_in[l].astype(F32)[0:half]
    window_attention(lat == n_lat - 1, window, gain, late, packed, mixed, done, out_ref)

    edge.wait_send()
    for third in range(THIRDS):
        for step in range(1, n_lev):
            tokens(third, step, False).wait_send()
    for which in range(2):
        cross(which, False).wait_send()
    for which in range(2):
        for step in range(1, steps + 1):
            for stream in streams(step):
                ring(which, stream, step, False).wait_send()
                exchange(which, stream, step, False).wait_send()


def on_device(tokens, query, base, key_w, value_w, out_w, gain, qkv_w, proj_w):
    n_lev, n_lat = lax.axis_size("lev"), lax.axis_size("lat")
    levels, rows, cols, width = tokens.shape
    token_rows = tokens.reshape(levels * rows, cols, width)
    gain_row = gain.reshape(1, width)
    operands = [
        pltpu.with_memory_space_constraint(operand, pltpu.HBM)
        for operand in (token_rows, query, base, key_w, value_w, out_w, gain_row, qkv_w, proj_w)
    ]
    length = LATENTS * PATCHES
    dma = pltpu.SemaphoreType.DMA
    return pl.pallas_call(
        functools.partial(kernel, n_lev, n_lat),
        out_shape=jax.ShapeDtypeStruct((LATENTS, rows, cols // n_lev, width), BF16),
        in_specs=[pl.BlockSpec(memory_space=pltpu.HBM)] * 9,
        out_specs=pl.BlockSpec(memory_space=pltpu.VMEM),
        scratch_shapes=[
            pltpu.VMEM((n_lat // 2, 2, SHARD, EARLY), BF16),
            pltpu.VMEM((n_lat // 2, 2, SHARD, LATE), BF16),
            pltpu.VMEM((THIRDS, n_lev, GROUPS, 16, width), BF16),
            pltpu.VMEM((THIRDS, n_lev, GROUPS, 16, width), BF16),
            pltpu.VMEM(token_rows.shape, BF16),
            pltpu.VMEM((4, cols + 8, width), F32),
            pltpu.VMEM(query.shape, BF16),
            pltpu.VMEM(base.shape, BF16),
            pltpu.VMEM(key_w.shape, BF16),
            pltpu.VMEM(gain_row.shape, F32),
            pltpu.VMEM((n_lev, GROUPS, 16, INNER), BF16),
            pltpu.VMEM((GROUPS, 128, 256), F32),
            pltpu.VMEM((THIRDS, LATENTS, PART, INNER), F32),
            pltpu.VMEM((LATENTS, PATCHES, width), F32),
            pltpu.VMEM((LATENTS, 48, width), BF16),
            pltpu.VMEM((LATENTS, 48, width), BF16),
            pltpu.VMEM((length, width), F32),
            pltpu.VMEM((length, 3 * width), BF16),
            pltpu.VMEM((length, width), BF16),
            pltpu.VMEM((length, width), F32),
            dma((9 + 2 * THIRDS,)),
            dma((THIRDS, n_lev)),
            dma((THIRDS, n_lev)),
            dma((4, n_lat // 4 + 1)),
            dma((4, n_lat // 4 + 1)),
            dma((4, n_lat // 4 + 1)),
            dma((4, n_lat // 4 + 1)),
            dma((2,)),
            dma((2,)),
            dma((2,)),
        ],
        compiler_params=pltpu.CompilerParams(
            collective_id=0, has_side_effects=True, vmem_limit_bytes=44 * 1024 * 1024
        ),
        cost_estimate=pl.CostEstimate(
            flops=6_000_000_000, bytes_accessed=8_000_000, transcendentals=1_000_000
        ),
    )(*operands)


def solution(mesh):
    placed = (
        P("lev", "lat", None, None),
        P(),
        P(),
        P("lat", None),
        P("lat", None),
        P("lat", None),
        P(),
        P("lat", None),
        P("lat", None),
    )
    return jax.shard_map(
        on_device,
        mesh=mesh,
        in_specs=placed,
        out_specs=P(None, "lat", "lev", None),
        check_vma=False,
    )
```

```python
import functools

import jax
import jax.numpy as jnp
from jax import lax
from jax.experimental import pallas as pl
from jax.experimental.pallas import tpu as pltpu
from jax.sharding import PartitionSpec as P

MESH = pl.DeviceIdType.MESH
F32 = jnp.float32
BF16 = jnp.bfloat16

HEAD_DIM = 64
LHEADS = 16
LATENTS = 3
WIN_R = 6
WIN_C = 12
WIDTH = 512
INNER = 1024
PATCHES = WIN_R * WIN_C
SHARD = 16
THIRDS = 3
PART = PATCHES // THIRDS
GROUPS = PART // 8
C_V, EARLY = 128, 1152
C_O, LATE = 512, 1536


def dot(a, b):
    return jnp.dot(a, b, preferred_element_type=F32)


def dot_t(a, b):
    return lax.dot_general(a, b, (((1,), (1,)), ((), ())), preferred_element_type=F32)


def iota(shape, dim):
    return lax.broadcasted_iota(jnp.int32, shape, dim)


def columns_of(gathered, start, stop):
    parts = [gathered[:, side, :, start:stop] for side in range(2)]
    return jnp.concatenate([p.reshape(-1, stop - start) for p in parts], axis=0)


def fold_query(query, key_rows):
    own_head = iota((LHEADS, INNER), 0) == iota((LHEADS, INNER), 1) // HEAD_DIM
    spread = [jnp.where(own_head, query[l : l + 1, :].astype(F32), 0.0) for l in range(LATENTS)]
    spread.append(jnp.zeros((64 - LATENTS * LHEADS, INNER), F32))
    spread = jnp.concatenate(spread * 2, axis=0).astype(BF16)
    folded = dot_t(key_rows[...], spread) * (HEAD_DIM**-0.5)
    high = folded.astype(BF16).astype(F32)
    low = folded - high
    return jnp.where(iota(folded.shape, 1) < 64, high, low).astype(BF16)


def regroup_tokens(third, devices, token_rows, floats, outgoing):
    cols = devices * WIN_C
    for k in range(4):
        row = (k // 2) * WIN_R + 2 * third + k % 2
        floats[k, 0:cols] = token_rows[row].astype(F32)
        floats[k, cols : cols + 8] = token_rows[row, 0:16].astype(F32)[0:8]
    for i in range(devices):
        first = i * WIN_C + WIN_C // 2
        cut = [floats[k, first : first + WIN_C] for k in range(4)]
        levels = [
            jnp.concatenate(cut[2 * l : 2 * l + 2], axis=0).reshape(GROUPS, 8, WIDTH)
            for l in range(2)
        ]
        for g in range(GROUPS):
            block = jnp.concatenate([levels[l][g] for l in range(2)], axis=0)
            outgoing[third, i, g] = block.astype(BF16)


def level_attention(third, arrived, early, values, turned, attn):
    devices = arrived.shape[1]
    rows = arrived[third].reshape(devices * 2 * PART, WIDTH)
    both = dot(rows, columns_of(early, 0, C_V))
    for c in range(2):
        found = dot(rows, columns_of(early, C_V + c * 512, C_V + c * 512 + 512)).astype(BF16)
        values[:, :, :, c * 512 : c * 512 + 512] = found.reshape(devices, GROUPS, 16, 512)
    both = both + jnp.concatenate([both[:, 64:], both[:, :64]], axis=1)
    scores = both.reshape(devices, GROUPS, 2, 8, 128)
    own_patch = iota((8, 256), 0) == lax.rem(iota((8, 256), 1), 8)
    head_of = iota((8, 256), 1) // HEAD_DIM
    for g in range(GROUPS):
        level = scores[:, g].reshape(2 * devices, 8, 128)
        weights = jnp.exp(level - jnp.max(level, axis=0, keepdims=True))
        weights = weights * (1.0 / jnp.sum(weights, axis=0, keepdims=True))
        turned[g] = weights.reshape(256, 128).T
        for quad in range(LHEADS // 4):
            spread = []
            for l in range(LATENTS):
                for h in range(4):
                    at = l * LHEADS + quad * 4 + h
                    row = jnp.broadcast_to(turned[g, at : at + 1, :], (8, 256))
                    spread.append(jnp.where(own_patch, row, 0.0))
            spread = jnp.concatenate(spread, axis=0).astype(BF16)
            v = values[:, g, :, quad * 256 : quad * 256 + 256].reshape(256, 256)
            sums = dot(spread, v).reshape(LATENTS, 4, 8, 256)
            for l in range(LATENTS):
                own = jnp.zeros((8, 256), F32)
                for h in range(4):
                    own = jnp.where(head_of == h, sums[l, h], own)
                attn[third, l, g * 8 : g * 8 + 8, quad * 256 : quad * 256 + 256] = own


def make_latents(thirds, attn, base, late, latents):
    parts = []
    for side in range(2):
        halves = [late[:, side, 1, :, C_O + c * 512 : C_O + c * 512 + 512] for c in range(2)]
        parts.append(jnp.stack(halves, axis=1).reshape(INNER // 2, WIDTH))
    weight = jnp.concatenate(parts, axis=0)
    count = len(thirds) * LATENTS
    rows = attn[thirds[0] : thirds[-1] + 1].reshape(count * PART, INNER).astype(BF16)
    mixed = dot(rows, weight).reshape(count, PART, WIDTH)
    for k, third in enumerate(thirds):
        for l in range(LATENTS):
            row = mixed[k * LATENTS + l] + base[l : l + 1, :].astype(F32)
            latents[l, third * PART : (third + 1) * PART] = row.astype(BF16).astype(F32)


def window_attention(last, window, gain, late, packed, mixed, done, out_ref):
    length = LATENTS * PATCHES
    x = window[...]
    center = jnp.mean(x, axis=-1, keepdims=True)
    moved = x - center
    spread = jnp.mean(moved * moved, axis=-1, keepdims=True)
    normed = (moved * lax.rsqrt(spread + 1e-05) * gain[...]).astype(BF16)
    for c in range(2):
        weight = columns_of(late.at[:, :, 0], c * 768, c * 768 + 768)
        packed[:, c * 768 : c * 768 + 768] = dot(normed, weight).astype(BF16)
    half = PATCHES // 2

    def region(dim):
        return lax.rem(iota((length, length), dim), PATCHES) >= half

    apart = jnp.logical_and(region(0) != region(1), last)
    bias = jnp.where(apart, -1e30, 0.0)
    first = iota((length, 128), 1) < HEAD_DIM

    for i in range(WIDTH // 128):
        at = i * 128
        q = packed[:, at : at + 128].astype(F32) * (HEAD_DIM**-0.5)
        k = packed[:, WIDTH + at : WIDTH + at + 128]
        v = packed[:, 2 * WIDTH + at : 2 * WIDTH + at + 128]
        outs = []
        for side in (first, jnp.logical_not(first)):
            s = dot_t(jnp.where(side, q, 0.0).astype(BF16), k) + bias
            w = jnp.exp(s - jnp.max(s, axis=-1, keepdims=True))
            w = (w * (1.0 / jnp.sum(w, axis=-1, keepdims=True))).astype(BF16)
            outs.append(dot(w, v))
        mixed[:, at : at + 128] = jnp.where(first, outs[0], outs[1]).astype(BF16)
    for c in range(2):
        weight = columns_of(late.at[:, :, 1], c * 256, c * 256 + 256)
        done[:, c * 256 : c * 256 + 256] = x[:, c * 256 : c * 256 + 256] + dot(mixed[...], weight)
    for l in range(LATENTS):
        for r in range(WIN_R):
            at = l * PATCHES + r * WIN_C
            out_ref[l, r] = done[at : at + WIN_C, :].astype(BF16)


def kernel(
    n_lev,
    n_lat,
    tok_hbm,
    q_hbm,
    base_hbm,
    kw_hbm,
    vw_hbm,
    ow_hbm,
    gain_hbm,
    qkvw_hbm,
    pw_hbm,
    out_ref,
    early,
    late,
    arrived,
    outgoing,
    token_rows,
    floats,
    query,
    base,
    key_rows,
    gain,
    values,
    turned,
    attn,
    latents,
    edge_out,
    edge_in,
    window,
    packed,
    mixed,
    done,
    load_sems,
    tok_send,
    tok_recv,
    ring_send,
    ring_recv,
    core_send,
    core_recv,
    hop_send,
    hop_recv,
    edge_sems,
):
    lev, lat = lax.axis_index("lev"), lax.axis_index("lat")
    depth = n_lat // 2
    side, z = lax.div(lat, depth), lax.rem(lat, depth)
    moves = []
    for third in range(THIRDS):
        for l in range(2):
            rows = pl.ds(l * WIN_R + 2 * third, 2)
            moves.append((tok_hbm.at[rows], token_rows.at[rows]))
    moves += [(q_hbm, query), (kw_hbm, key_rows), (base_hbm, base), (gain_hbm, gain)]
    moves += [
        (vw_hbm, early.at[z, side, :, C_V:EARLY]),
        (qkvw_hbm, late.at[z, side, 0]),
        (pw_hbm, late.at[z, side, 1, :, 0:C_O]),
        (ow_hbm.at[0:16], late.at[z, side, 1, :, C_O : C_O + 512]),
        (ow_hbm.at[16:32], late.at[z, side, 1, :, C_O + 512 : LATE]),
    ]
    loads = [pltpu.make_async_copy(*m, load_sems.at[i]) for i, m in enumerate(moves)]
    first = loads[:2] + loads[2 * THIRDS :]
    for load in first + loads[2 : 2 * THIRDS]:
        load.start()

    core = lax.rem(lev, 2)
    sibling = lev + 1 - 2 * core

    def at_z(step):
        return lax.rem(z + step + depth, depth)

    up, down = side * depth + at_z(1), side * depth + at_z(-1)
    across = (1 - side) * depth + z
    north, south = lax.rem(lat + n_lat - 1, n_lat), lax.rem(lat + 1, n_lat)

    barrier = pltpu.get_barrier_semaphore()
    for peer in (up, down, across, north, south):
        pl.semaphore_signal(
            barrier, inc=1, device_id={"lev": lev, "lat": peer}, device_id_type=MESH
        )
    for k in range(1, n_lev):
        peer = lax.rem(lev + k, n_lev)
        pl.semaphore_signal(
            barrier, inc=1, device_id={"lev": peer, "lat": lat}, device_id_type=MESH
        )

    def regroup(third):
        loads[2 * third].wait()
        loads[2 * third + 1].wait()
        regroup_tokens(third, n_lev, token_rows, floats, outgoing)

    regroup(0)
    for load in first[2:]:
        load.wait()
    early[z, side, :, 0:C_V] = fold_query(query, key_rows)
    pl.semaphore_wait(barrier, 5 + n_lev - 1)

    kinds = range(3)

    def part(which, at, there):
        return early.at[at, there] if which == 0 else late.at[at, there, which - 1]

    steps = depth // 2
    way = 1 - 2 * core
    onward = side * depth + at_z(way)

    def side_of(stream, step):
        if step == steps:
            return side + core * (1 - 2 * side)
        return side if stream == 0 else 1 - side

    def ring(which, stream, step, arriving):
        at = at_z(-way * (step if arriving else step - 1)), side_of(stream, step)
        return pltpu.make_async_remote_copy(
            src_ref=part(which, *at),
            dst_ref=part(which, *at),
            send_sem=ring_send.at[which * 2 + stream, step],
            recv_sem=ring_recv.at[which * 2 + stream, step],
            device_id={"lev": lev, "lat": onward},
            device_id_type=MESH,
        )

    def exchange(which, stream, step, arriving):
        there = side_of(stream, step)
        if arriving and step == steps:
            there = 1 - there
        at = at_z(way * step if arriving else -way * step), there
        return pltpu.make_async_remote_copy(
            src_ref=part(which, *at),
            dst_ref=part(which, *at),
            send_sem=core_send.at[which * 2 + stream, step],
            recv_sem=core_recv.at[which * 2 + stream, step],
            device_id={"lev": sibling, "lat": lat},
            device_id_type=MESH,
        )

    def streams(step):
        return range(1 if step == steps else 2)

    def cross(which, arriving):
        at = 1 - side if arriving else side
        return pltpu.make_async_remote_copy(
            src_ref=part(which, z, at),
            dst_ref=part(which, z, at),
            send_sem=hop_send.at[which],
            recv_sem=hop_recv.at[which],
            device_id={"lev": lev, "lat": across},
            device_id_type=MESH,
        )

    def tick(some, step):
        for stream in streams(step):
            for which in some:
                ring(which, stream, step, True).wait_recv()
                if step + 1 < steps:
                    ring(which, stream, step + 1, False).start()
                elif step < steps and stream == 1:
                    ring(which, 0, steps, False).start()
                exchange(which, stream, step, False).start()

    def all_shared(which):
        for step in range(1, steps + 1):
            for stream in streams(step):
                exchange(which, stream, step, True).wait_recv()

    def tokens(third, step, arriving):
        peer = lax.rem(lev + (n_lev - step if arriving else step), n_lev)
        return pltpu.make_async_remote_copy(
            src_ref=outgoing.at[third, peer],
            dst_ref=arrived.at[third, peer if arriving else lev],
            send_sem=tok_send.at[third, step],
            recv_sem=tok_recv.at[third, step],
            device_id={"lev": peer, "lat": lat},
            device_id_type=MESH,
        )

    def own(third):
        return pltpu.make_async_copy(
            outgoing.at[third, lev], arrived.at[third, lev], tok_send.at[third, 0]
        )

    def send_tokens(third):
        for step in range(1, n_lev):
            tokens(third, step, False).start()
        own(third).start()

    def tokens_here(third):
        own(third).wait()
        for step in range(1, n_lev):
            tokens(third, step, True).wait_recv()

    for which in kinds:
        cross(which, False).start()
        ring(which, 0, 1, False).start()
    send_tokens(0)
    for which in kinds:
        cross(which, True).wait_recv()
        ring(which, 1, 1, False).start()
    regroup(1)
    send_tokens(1)
    tick(kinds, 1)
    regroup(2)
    send_tokens(2)
    for step in range(2, steps):
        tick(kinds, step)
    tick((0,), steps)
    all_shared(0)

    for third in range(THIRDS):
        tokens_here(third)
        level_attention(third, arrived, early, values, turned, attn)
        if third == 0:
            tick((1, 2), steps)
        if third == 1:
            all_shared(1)
            all_shared(2)
            make_latents((0, 1), attn, base, late, latents)
            edge_out[...] = latents[:, 0:48, :].astype(BF16)
            edge = pltpu.make_async_remote_copy(
                src_ref=edge_out,
                dst_ref=edge_in,
                send_sem=edge_sems.at[0],
                recv_sem=edge_sems.at[1],
                device_id={"lev": lev, "lat": north},
                device_id_type=MESH,
            )
            edge.start()
    make_latents((2,), attn, base, late, latents)

    half = PATCHES // 2
    for l in range(LATENTS):
        window[l * PATCHES : l * PATCHES + half] = latents[l, half:PATCHES]
    edge.wait_recv()
    for l in range(LATENTS):
        window[l * PATCHES + half : (l + 1) * PATCHES] = edge_in[l].astype(F32)[0:half]
    window_attention(lat == n_lat - 1, window, gain, late, packed, mixed, done, out_ref)

    edge.wait_send()
    for third in range(THIRDS):
        for step in range(1, n_lev):
            tokens(third, step, False).wait_send()
    for which in kinds:
        cross(which, False).wait_send()
    for which in kinds:
        for step in range(1, steps + 1):
            for stream in streams(step):
                ring(which, stream, step, False).wait_send()
                exchange(which, stream, step, False).wait_send()


def on_device(tokens, query, base, key_w, value_w, out_w, gain, qkv_w, proj_w):
    n_lev, n_lat = lax.axis_size("lev"), lax.axis_size("lat")
    levels, rows, cols, width = tokens.shape
    token_rows = tokens.reshape(levels * rows, cols, width)
    gain_row = gain.reshape(1, width)
    operands = [
        pltpu.with_memory_space_constraint(operand, pltpu.HBM)
        for operand in (token_rows, query, base, key_w, value_w, out_w, gain_row, qkv_w, proj_w)
    ]
    length = LATENTS * PATCHES
    dma = pltpu.SemaphoreType.DMA
    return pl.pallas_call(
        functools.partial(kernel, n_lev, n_lat),
        out_shape=jax.ShapeDtypeStruct((LATENTS, rows, cols // n_lev, width), BF16),
        in_specs=[pl.BlockSpec(memory_space=pltpu.HBM)] * 9,
        out_specs=pl.BlockSpec(memory_space=pltpu.VMEM),
        scratch_shapes=[
            pltpu.VMEM((n_lat // 2, 2, SHARD, EARLY), BF16),
            pltpu.VMEM((n_lat // 2, 2, 2, SHARD, LATE), BF16),
            pltpu.VMEM((THIRDS, n_lev, GROUPS, 16, width), BF16),
            pltpu.VMEM((THIRDS, n_lev, GROUPS, 16, width), BF16),
            pltpu.VMEM(token_rows.shape, BF16),
            pltpu.VMEM((4, cols + 8, width), F32),
            pltpu.VMEM(query.shape, BF16),
            pltpu.VMEM(base.shape, BF16),
            pltpu.VMEM(key_w.shape, BF16),
            pltpu.VMEM(gain_row.shape, F32),
            pltpu.VMEM((n_lev, GROUPS, 16, INNER), BF16),
            pltpu.VMEM((GROUPS, 128, 256), F32),
            pltpu.VMEM((THIRDS, LATENTS, PART, INNER), F32),
            pltpu.VMEM((LATENTS, PATCHES, width), F32),
            pltpu.VMEM((LATENTS, 48, width), BF16),
            pltpu.VMEM((LATENTS, 48, width), BF16),
            pltpu.VMEM((length, width), F32),
            pltpu.VMEM((length, 3 * width), BF16),
            pltpu.VMEM((length, width), BF16),
            pltpu.VMEM((length, width), F32),
            dma((9 + 2 * THIRDS,)),
            dma((THIRDS, n_lev)),
            dma((THIRDS, n_lev)),
            dma((6, n_lat // 4 + 1)),
            dma((6, n_lat // 4 + 1)),
            dma((6, n_lat // 4 + 1)),
            dma((6, n_lat // 4 + 1)),
            dma((3,)),
            dma((3,)),
            dma((2,)),
        ],
        compiler_params=pltpu.CompilerParams(
            collective_id=0, has_side_effects=True, vmem_limit_bytes=44 * 1024 * 1024
        ),
        cost_estimate=pl.CostEstimate(
            flops=6_000_000_000, bytes_accessed=8_000_000, transcendentals=1_000_000
        ),
    )(*operands)


def solution(mesh):
    placed = (
        P("lev", "lat", None, None),
        P(),
        P(),
        P("lat", None),
        P("lat", None),
        P("lat", None),
        P(),
        P("lat", None),
        P("lat", None),
    )
    return jax.shard_map(
        on_device,
        mesh=mesh,
        in_specs=placed,
        out_specs=P(None, "lat", "lev", None),
        check_vma=False,
    )
```
